128 devices in a mesh: row: 8 (over x_lo, y), col: 16 (over x_hi, z, core).
Axes of the slice: x: 4 (x_hi: 2, x_lo: 2; x = x_hi * 2 + x_lo), y: 4, z: 4, core: 2. Of those that a mesh axis runs over, the one named last changes fastest.
Arguments:
- positions: float32 [3, 393216], P(None, ('row', 'col')), may hold values from -1 to 1
- normals: float32 [3, 393216], P(None, ('row', 'col')), may hold values from -4 to 4
- patch_extents: float32 [393216], P(('row', 'col')), may hold values from 0.02 to 0.2
- mirrored_fraction: float32 [393216], P(('row', 'col')), may hold values from 0.1 to 0.9
- inner_emission_power: float32 [393216], P(('row', 'col')), may hold values from 0.1 to 1
- radiosity: float32 [393216], P(('row', 'col')), may hold values from 0.2 to 2
- basis: float32 [8, 393216], P(None, ('row', 'col')), may hold values from -6 to 6
- recv_blocks: int32 [8, 16, 512], P('row', 'col'), may hold values from 0 to 191
- emit_blocks: int32 [8, 16, 512], P('row', 'col'), may hold values from 0 to 383
- vis_count: int32 [8, 16], P('row', 'col'), may hold values from 128 to 512, as said below
- owner: int32 [393216, 1], P(('row', 'col')), may hold values from 0 to 127; in each aligned block of 3072 rows (0 to 3071, 3072 to 6143, ...) at most 96 rows name the same one
- local_elem: int32 [393216], P(('row', 'col')), may hold values from 0 to 2047
Outputs:
- new_vector: float32 [393216], P(('row', 'col'))
- hessen: float32 [9], replicated
- element_loads: float32 [262144], P(('row', 'col'))
The draws below stay inside these ranges and needn't reach their ends.
Inputs may be any that keep to these rules, and one draw needn't show every extreme that they name: `vis_count`: some device has 512 live entries in every draw. Among the patches of one device no owner is named more than 96 times; that many is reached.
All inputs are finite; a program needn't handle non-finite values.
Results may differ from the reference program's by a relative error of at most 0.0003.
Values sent between devices are 32-bit elements; how exact they have to be, the bound alone decides.
No kernel may reach another device: no remote copies, remote signals or barrier semaphores. Data moves between devices by JAX's collectives and lax.ppermute only.
A program may use at most 64 MiB of HBM per device.

```python
import math
import jax
import jax.numpy as jnp
import numpy as np
from jax import lax

P_DEV = 3072
VIS = 512
K = 8
E_DEV = 2048
NP = 393216
RB = 192
EB = 384
ELEMS = 262144
CAP = 96
N_ROW = 8
N_COL = 16
DEVICES = 128


def draw_vis_count(key, part):
    key = jax.random.fold_in(key, 11)
    first_key, later_sorting_criterion = jax.random.split(key)
    counts = jax.random.randint(first_key, (N_ROW * N_COL,), VIS // 4, VIS + 1)
    fullest = jax.random.randint(later_sorting_criterion, (), 0, N_ROW * N_COL)
    counts = jnp.where(jnp.arange(N_ROW * N_COL) == fullest, VIS, counts)
    return counts.reshape(N_ROW, N_COL).astype(jnp.int32)


def place_ends(drawn, key, least, top_value):
    longest = drawn.shape.index(max(drawn.shape))
    spots = []
    for shift in (0, 1):
        where = [jax.random.randint(jax.random.fold_in(key, axis), (), 0, length) for axis, length in enumerate(drawn.shape)]
        where[longest] = (where[longest] + shift) % drawn.shape[longest]
        spots.append(tuple(where))
    return drawn.at[spots[0]].set(least).at[spots[1]].set(top_value)


def block_levels(key, shape, cuts, least, top_value):
    factor_of, own = 1.0, jax.random.fold_in(key, 6)
    for position, shards_of in cuts:
        steps = jnp.exp(jax.random.uniform(jax.random.fold_in(own, position), (shards_of,), jnp.float32, least / len(cuts), top_value / len(cuts)))
        factor_of = factor_of * jnp.repeat(steps, shape[position] // shards_of).reshape([-1 if axis == position else 1 for axis in range(len(shape))])
    return factor_of


def shared_out(key, own, number, rows, number_of, top, bound, lean):
    ranking = jax.random.permutation(key, number_of)
    heavy_load, usual = load_shares(number_of, rows * top, bound, lean, True), load_shares(number_of, rows * top, bound, lean, False)
    places = jnp.arange(number_of)

    def named(lengths, rotation):
        used = int((lengths > 0).sum())
        fixed = max(1, used // 4)
        shifted = fixed + (places - fixed + rotation * (used - fixed)) % max(1, number_of - fixed)
        return jnp.zeros((number_of,), jnp.int32).at[ranking[jnp.where(places < fixed, places, shifted)]].set(jnp.asarray(lengths, jnp.int32))

    lengths = jnp.where(number % 4 == 0, named(heavy_load, number // 4), named(usual, number - number // 4 - 1))
    mixed = jax.random.permutation(jax.random.fold_in(own, 3), number_of)
    donor, taker = mixed[0:number_of // 2 * 2:2], mixed[1:number_of // 2 * 2:2]
    room = jnp.minimum(lengths[donor] - 1, bound - lengths[taker]) // 2
    room = jnp.where((donor == ranking[0]) | (taker == ranking[0]) | (lengths[taker] == 0), 0, jnp.maximum(room, 0))
    shifted = jax.random.randint(jax.random.fold_in(own, 4), (number_of // 2,), 0, 1 << 20) % (room + 1)
    lengths = lengths.at[donor].add(-shifted).at[taker].add(shifted)
    members = jnp.searchsorted(jnp.cumsum(lengths), jnp.arange(rows * top), side="right").astype(jnp.int32)
    grid = members.reshape(top, rows).T
    grid = grid[jax.random.permutation(jax.random.fold_in(own, 1), rows)]
    rotation = jax.random.randint(jax.random.fold_in(own, 2), (rows, 1), 0, top)
    return jnp.take_along_axis(grid, (jnp.arange(top)[None, :] + rotation) % top, axis=1)


def load_shares(number_of, total, limit, skew, full):
    portions = [(1 << 20) // math.isqrt(standing ** skew) + 1 for standing in range(1, number_of + 1)]
    largest = limit if full else min(limit, max(-(-total // number_of), total * portions[0] // sum(portions)))
    least = 1 if total - largest >= number_of - 1 else 0
    given, spare = [largest] + [least] * (number_of - 1), total - largest - least * (number_of - 1)
    while spare > 0:
        free = [i for i in range(1, number_of) if given[i] < largest] or [i for i in range(1, number_of) if given[i] < limit]
        mass, remaining = sum([portions[i] for i in free]), spare
        for i in free:
            addition = min(limit - given[i], max(1, remaining * portions[i] // mass), spare)
            given[i] = given[i] + addition
            spare = spare - addition
    return np.array(given)


def normal_values(key, extent, scale, reach, cuts=(), kind=jnp.bfloat16):
    array = scale * jax.random.normal(key, extent, jnp.float32)
    if cuts:
        array = array * block_levels(key, extent, cuts, -0.22, 0.18)
    return jnp.clip(array, -reach, reach).astype(kind)


def setup_inputs(seed: int = 0) -> dict:
    splits = jax.random.split(jax.random.key(seed), 13)
    positions = jnp.clip(jax.random.uniform(splits[0], (3, NP), jnp.float32, -1.0, 1.0) * block_levels(splits[0], (3, NP), ((1, 128),), -0.4, 0.0), -1.0, 1.0)
    normals = normal_values(splits[1], (3, NP), 1.0, 4.0, ((1, 128),), jnp.float32)
    patch_extents = jnp.clip(jnp.exp(math.log(0.2) - 2.3025851 * jax.random.uniform(splits[2], (NP,), jnp.float32) ** block_levels(splits[2], (NP,), ((0, 128),), -0.2, 0.2)), 0.02, 0.2)
    mirrored_fraction = jnp.clip(0.1 + 0.79999997 * jax.random.uniform(splits[3], (NP,), jnp.float32) ** block_levels(splits[3], (NP,), ((0, 128),), -0.2, 0.2), 0.1, 0.9)
    inner_emission_power = jnp.clip(jnp.exp(math.log(1.0) - 2.3025851 * jax.random.uniform(splits[4], (NP,), jnp.float32) ** block_levels(splits[4], (NP,), ((0, 128),), -0.2, 0.2)), 0.1, 1.0)
    radiosity = jnp.clip(0.2 + 1.8 * jax.random.uniform(splits[5], (NP,), jnp.float32) ** block_levels(splits[5], (NP,), ((0, 128),), -0.2, 0.2), 0.2, 2.0)
    basis = normal_values(splits[6], (K, NP), 1.0, 6.0, ((1, 128),), jnp.float32)
    recv_blocks = place_ends(jax.random.randint(splits[7], (N_ROW, N_COL, VIS), 0, RB), jax.random.fold_in(splits[7], 1), 0, RB - 1).astype(jnp.int32)
    emit_blocks = place_ends(jax.random.randint(splits[8], (N_ROW, N_COL, VIS), 0, EB), jax.random.fold_in(splits[8], 1), 0, EB - 1).astype(jnp.int32)
    vis_count = draw_vis_count(jax.random.fold_in(splits[12], 71), 0)
    owner_keys = jax.random.split(jax.random.fold_in(splits[10], 1), NP // P_DEV)
    owner_turns = jax.random.permutation(jax.random.fold_in(splits[10], 3), NP // P_DEV)
    owner = jax.vmap(lambda own, number: shared_out(jax.random.fold_in(splits[10], 2), own, number, P_DEV, DEVICES, 1, CAP, 2))(owner_keys, owner_turns).reshape((NP, 1))
    local_elem = place_ends(jax.random.randint(splits[11], (NP,), 0, E_DEV), jax.random.fold_in(splits[11], 1), 0, E_DEV - 1).astype(jnp.int32)
    return dict(positions=positions, normals=normals, patch_extents=patch_extents, mirrored_fraction=mirrored_fraction, inner_emission_power=inner_emission_power, radiosity=radiosity, basis=basis, recv_blocks=recv_blocks, emit_blocks=emit_blocks, vis_count=vis_count, owner=owner, local_elem=local_elem)


def view_terms(receiver, emitter, vectors):
    offset = emitter[0:3, :, None, :] - receiver[0:3, :, :, None]
    facing = jnp.maximum(lax.optimization_barrier(jnp.sum(receiver[3:6, :, :, None] * offset, axis=0)), 0.0)
    destination_index = jnp.maximum(-lax.optimization_barrier(jnp.sum(emitter[3:6, :, None, :] * offset, axis=0)), 0.0)
    area_row = emitter[6][:, None, :]
    spread = lax.optimization_barrier(jnp.sum(offset * offset, axis=0)) + area_row
    factor = facing * destination_index * area_row / (jnp.pi * spread * spread)
    return jnp.einsum('gre,kge->kgr', factor, vectors, precision=lax.Precision.HIGHEST)

def group_sum(totals, recv_tiles, emit_tiles, receiver_selection, emit_pick, weight_pick):
    recv_part = jnp.take(recv_tiles, receiver_selection, axis=1)
    emit_part = jnp.take(emit_tiles, emit_pick, axis=1)
    contrib = view_terms(recv_part, emit_part[0:7], emit_part[7:9]) * weight_pick[None, :, None]
    return totals.at[:, receiver_selection].add(contrib)

def reference(positions, normals, patch_extents, mirrored_fraction, inner_emission_power, radiosity, basis, recv_blocks, emit_blocks, vis_count, owner, local_elem):
    devices = N_ROW * N_COL
    krylov = basis[K - 1]
    receiver = jnp.concatenate([positions, normals], axis=0).reshape(6, N_ROW, N_COL, P_DEV)
    emitter = jnp.concatenate([positions, normals, patch_extents[None], radiosity[None], krylov[None]], axis=0)
    emitter = emitter.reshape(9, N_ROW, N_COL * P_DEV // 128, 128)
    rounds = VIS // 16

    def per_device(carried, flat):
        row_at = (flat // N_COL).astype(jnp.int32)
        col_at = (flat % N_COL).astype(jnp.int32)
        recv_tiles = lax.dynamic_index_in_dim(receiver, col_at, 2, keepdims=False).reshape(6, N_ROW * P_DEV // 128, 128)
        emit_tiles = lax.dynamic_index_in_dim(emitter, row_at, 1, keepdims=False)
        recv_list = recv_blocks[row_at, col_at]
        emit_list = emit_blocks[row_at, col_at]
        live_mask = (jnp.arange(VIS, dtype=jnp.int32) < vis_count[row_at, col_at]).astype(jnp.float32)

        def advance(round_at, totals):
            begin = (round_at * 16).astype(jnp.int32)
            return group_sum(totals, recv_tiles, emit_tiles, lax.dynamic_slice_in_dim(recv_list, begin, 16), lax.dynamic_slice_in_dim(emit_list, begin, 16), lax.dynamic_slice_in_dim(live_mask, begin, 16))
        totals = lax.fori_loop(0, rounds, advance, jnp.zeros((2, N_ROW * P_DEV // 128, 128), jnp.float32))
        partial_value = totals.reshape(2, N_ROW, P_DEV)
        carried = carried.at[:, :, col_at, :].add(partial_value)
        return (carried, None)
    summed, _ = lax.scan(per_device, jnp.zeros((2, N_ROW, N_COL, P_DEV), jnp.float32), jnp.arange(devices, dtype=jnp.int32))
    summed = summed.reshape(2, NP)
    arriving_power_density = summed[0]
    scattered = summed[1]
    applied = krylov - mirrored_fraction * scattered
    projection_weights = jnp.dot(basis, applied, precision=lax.Precision.HIGHEST) / NP
    leftover_residual = applied - jnp.dot(projection_weights, basis, precision=lax.Precision.HIGHEST)
    length = jnp.sqrt(jnp.sum(leftover_residual * leftover_residual) / NP + 1e-06)
    new_vector = leftover_residual / length
    hessen = jnp.concatenate([projection_weights, length[None]])
    plate_kelvin_level = ((1.0 - mirrored_fraction) * arriving_power_density + inner_emission_power) ** 0.25
    boundary_warming_demand = 20.0 * patch_extents * plate_kelvin_level
    global_elem = (owner[:, 0] * E_DEV + local_elem).astype(jnp.int32)
    element_loads = jnp.zeros((ELEMS,), jnp.float32).at[global_elem].add(boundary_warming_demand)
    return (new_vector, hessen, element_loads)
```

```python
import functools
import math

import jax
import jax.numpy as jnp
from jax import lax
from jax.experimental import pallas as pl
from jax.experimental.pallas import tpu as pltpu
from jax.sharding import PartitionSpec as P

F32 = jnp.float32
BF16 = jnp.bfloat16
LANES = 128
E_DEV = 2048
NT = (((1,), (1,)), ((), ()))
TN = (((0,), (0,)), ((), ()))
VMEM = pl.BlockSpec(memory_space=pltpu.VMEM)
SMEM = pl.BlockSpec(memory_space=pltpu.SMEM)
LIMIT = 48 * 2**20


def split3(value):
    high = value.astype(BF16).astype(F32)
    rest = value - high
    middle = rest.astype(BF16).astype(F32)
    return high, middle, rest - middle


def call(body, out_shape, scratch=(), in_specs=None, name=None, cost=None):
    return pl.pallas_call(
        body,
        out_shape=out_shape,
        in_specs=in_specs,
        out_specs=jax.tree.map(lambda _: VMEM, out_shape),
        scratch_shapes=list(scratch),
        compiler_params=pltpu.CompilerParams(vmem_limit_bytes=LIMIT),
        cost_estimate=cost,
        name=name,
    )


def stage_kernel(tiles, n_col, n_row, pos, nor, area, rad, kry, emit, recv):
    x = [pos[k * tiles : (k + 1) * tiles] for k in range(3)]
    n = [nor[k * tiles : (k + 1) * tiles] for k in range(3)]
    a = area[...]
    b = rad[...]
    weight = a * b * (1.0 / math.pi)
    m = [weight * v for v in n]
    square = x[0] * x[0] + x[1] * x[1] + x[2] * x[2]
    emit_rows = x + m + [-(m[0] * x[0] + m[1] * x[1] + m[2] * x[2]), square + a]
    recv_rows = x + n + [-(n[0] * x[0] + n[1] * x[1] + n[2] * x[2]), square]
    ratio = kry[...] / b
    for c in range(n_col):
        base = c * 9 * tiles
        for f in range(8):
            emit[pl.ds(base + f, tiles, stride=8), :] = emit_rows[f]
        emit[base + 8 * tiles : base + 9 * tiles, :] = ratio
    for r in range(n_row):
        for f in range(8):
            recv[pl.ds(r * 8 * tiles + f, tiles, stride=8), :] = recv_rows[f]


def rank_kernel(tiles, owner, elem, basis, rank, slots, gram):
    sub = lax.broadcasted_iota(jnp.int32, (LANES, LANES), 0)
    lane = lax.broadcasted_iota(jnp.int32, (LANES, LANES), 1)
    upper = jnp.concatenate([(sub < lane).astype(BF16), jnp.ones((LANES, LANES), BF16)], 1)
    carry = jnp.zeros((LANES, LANES), F32)
    found = jnp.zeros((LANES, 2 * LANES), F32)
    for g in range(tiles):
        named = owner[g : g + 1, :] == sub
        hot = jnp.where(named, 1.0, 0.0)
        counts = jnp.dot(hot.astype(BF16), upper, preferred_element_type=F32)
        place = jnp.sum(hot * (counts[:, :LANES] + carry), axis=0, keepdims=True)
        carry = carry + counts[:, LANES:]
        place = place.astype(jnp.int32)
        rank[g : g + 1, :] = place
        index = elem[g : g + 1, :]
        high = (index >> 7).astype(F32)
        low = (index & 127).astype(F32)
        at = place == sub
        table = jnp.concatenate([jnp.where(at, high, 0.0), jnp.where(at, low, 0.0)], 0)
        found = found + lax.dot_general(
            hot.astype(BF16), table.astype(BF16), NT, preferred_element_type=F32
        )
    slots[...] = found[:, :LANES] * 128.0 + found[:, LANES:]
    lanes = lax.broadcasted_iota(jnp.int32, (1, LANES), 1)
    total = jnp.zeros((1, LANES), F32)
    at = 0
    for i in range(8):
        for j in range(i, 8):
            value = jnp.sum(
                basis[i * tiles : (i + 1) * tiles] * basis[j * tiles : (j + 1) * tiles],
                axis=(0, 1),
                keepdims=True,
            )
            total = total + jnp.where(lanes == at, value, 0.0)
            at += 1
    gram[...] = total


def pair_kernel(tiles, n_row, n_col, unroll, count, recv_list, emit_list, emit, recv, out, etab, wtab, wone, acc):
    row = lax.broadcasted_iota(jnp.int32, (8, LANES), 0)
    zero = jnp.zeros((8, LANES), F32)
    ones3 = jnp.where(row < 3, 1.0, 0.0)

    def recv_body(r, _):
        block = recv[pl.ds(pl.multiple_of(r * 8, 8), 8), :]
        parts = split3(block)
        facing, away, spread = [], [], []
        for k, part in enumerate(parts):
            one = 1.0 if k == 0 else 0.0
            facing.append(jnp.where(row < 3, pltpu.roll(part, 5, 0), 0.0))
            x_low = pltpu.roll(part, 3, 0)
            away.append(
                jnp.where(row < 3, 0.0, jnp.where(row < 6, x_low, jnp.where(row == 6, one, 0.0)))
            )
            spread.append(jnp.where(row < 3, -2.0 * part, jnp.where(row == 7, one, 0.0)))
        consts = []
        for f in (6, 7):
            h, m, l = (part[f : f + 1, :] for part in parts)
            consts.append(
                jnp.where(row == 0, h, jnp.where(row == 1, m, jnp.where(row == 2, l, 0.0)))
            )
        for k, (w, c) in enumerate(((facing, consts[0]), (away, zero), (spread, consts[1]))):
            h, m, l = w
            wtab[r, :, k * LANES : (k + 1) * LANES] = jnp.concatenate(
                [h, m, h, l, h, m, c, zero], 0
            ).astype(BF16)
        return 0

    lax.fori_loop(0, n_row * tiles, recv_body, 0, unroll=8)
    wone[...] = jnp.concatenate([zero] * 7 + [ones3], 0).astype(BF16)

    def emit_body(g, _):
        base = g * 9 * tiles
        for k in range(tiles):
            block = emit[pl.ds(pl.multiple_of(base + k * 8, 8), 8), :]
            h, m, l = split3(block)
            th, tm, tl = split3(emit[pl.ds(base + 8 * tiles + k, 1), :])
            tail = jnp.where(
                row == 0, th, jnp.where(row == 1, tm, jnp.where(row == 2, tl, 0.0))
            )
            etab[g * tiles + k] = jnp.concatenate([h, h, m, h, l, m, ones3, tail], 0).astype(BF16)
        return 0

    lax.fori_loop(0, n_col, emit_body, 0)
    acc[...] = jnp.zeros_like(acc)
    live = count[0]

    def fold(full):
        total = full[0:8]
        for k in range(1, LANES // 8):
            total = total + full[8 * k : 8 * k + 8]
        return total

    def pair(at):
        r = recv_list[at]
        e = emit_list[at]
        weights = jnp.concatenate([wtab[r], wone[...]], 1)
        g = lax.dot_general(etab[e], weights, TN, preferred_element_type=F32)
        facing = jnp.maximum(g[:, :LANES], 0.0)
        away = jnp.maximum(g[:, LANES : 2 * LANES], 0.0)
        spread = g[:, 2 * LANES : 3 * LANES]
        first = facing * away / (spread * spread)
        second = first * g[:, 3 * LANES :]
        return r, fold(first), fold(second)

    def step(i, _):
        found = [pair(i * unroll + k) for k in range(unroll)]
        for k, (r, first, second) in enumerate(found):
            keep = jnp.where(i * unroll + k < live, 1.0, 0.0)
            at = pl.multiple_of(r * 16, 16)
            acc[pl.ds(at, 8), :] = acc[pl.ds(at, 8), :] + first * keep
            acc[pl.ds(at + 8, 8), :] = acc[pl.ds(at + 8, 8), :] + second * keep
        return 0

    lax.fori_loop(0, (live + unroll - 1) // unroll, step, 0)
    for q in range(n_row):
        for v in range(2):
            total = acc[pl.ds(q * tiles * 16 + v * 8, tiles, stride=16), :]
            for s in range(1, 8):
                total = total + acc[pl.ds(q * tiles * 16 + v * 8 + s, tiles, stride=16), :]
            out[q * 2 * tiles + v * tiles : q * 2 * tiles + (v + 1) * tiles, :] = total


def load_kernel(tiles, n_row, part, basis, mirrored, inner, area, owner, rank, slots, gram, message, damped):
    sub = lax.broadcasted_iota(jnp.int32, (LANES, LANES), 0)
    irradiance = part[0:tiles, :]
    scattered = part[tiles : 2 * tiles, :]
    for q in range(1, n_row):
        irradiance = irradiance + part[2 * q * tiles : (2 * q + 1) * tiles, :]
        scattered = scattered + part[(2 * q + 1) * tiles : (2 * q + 2) * tiles, :]
    fraction = mirrored[...]
    lost = fraction * scattered
    damped[...] = lost
    power = (1.0 - fraction) * irradiance + inner[...]
    load = 20.0 * area[...] * jnp.sqrt(jnp.sqrt(power))
    parts = split3(load)
    found = jnp.zeros((LANES, LANES), F32)
    for g in range(tiles):
        hot = jnp.where(owner[g : g + 1, :] == sub, 1.0, 0.0).astype(BF16)
        at = rank[g : g + 1, :] == sub
        table = jnp.concatenate([jnp.where(at, v[g : g + 1, :], 0.0) for v in parts], 1)
        found = found + lax.dot_general(
            jnp.concatenate([hot] * 3, 1), table.astype(BF16), NT, preferred_element_type=F32
        )
    lanes = lax.broadcasted_iota(jnp.int32, (1, LANES), 1)
    stats = jnp.zeros((1, LANES), F32)
    for k in range(9):
        other = basis[k * tiles : (k + 1) * tiles, :] if k < 8 else lost
        value = jnp.sum(other * lost, axis=(0, 1), keepdims=True)
        stats = stats + jnp.where(lanes == 96 + k, value, 0.0)
    g = gram[...]
    shifted = pltpu.roll(jnp.broadcast_to(g, (8, LANES)), 105, 1)[0:1]
    stats = jnp.where(lanes >= 105, shifted, stats)
    more = pltpu.roll(jnp.broadcast_to(g, (8, LANES)), 73, 1)[0:1]
    keep = lax.broadcasted_iota(jnp.int32, (LANES, LANES), 1) < 96
    message[pl.ds(0, LANES, stride=2), :] = jnp.where(keep, found, stats)
    message[pl.ds(1, LANES, stride=2), :] = jnp.where(keep, slots[...], more)


def finish_kernel(tiles, cells, arrived, basis, damped, vector, hessen, loads, value_rows, index_rows):
    values = arrived[pl.ds(0, LANES, stride=2), :]
    second = arrived[pl.ds(1, LANES, stride=2), :]
    top = jnp.sum(values, axis=0, keepdims=True)
    low = jnp.sum(second, axis=0, keepdims=True)
    inner = [top[:, 96 + k : 97 + k] for k in range(8)]
    lost_square = top[:, 104:105]
    gram = {}
    at = 0
    for i in range(8):
        for j in range(i, 8):
            lane = 105 + at
            gram[i, j] = top[:, lane : lane + 1] if lane < 128 else low[:, lane - 32 : lane - 31]
            gram[j, i] = gram[i, j]
            at += 1
    scale = 1.0 / cells
    coeffs = [(gram[7, k] - inner[k]) * scale for k in range(8)]
    left = [(1.0 if k == 7 else 0.0) - coeffs[k] for k in range(8)]
    square = lost_square
    for i in range(8):
        line = gram[i, i] * left[i] - 2.0 * inner[i]
        for j in range(i + 1, 8):
            line = line + 2.0 * gram[i, j] * left[j]
        square = square + line * left[i]
    length = jnp.sqrt(jnp.maximum(square, 0.0) * scale + 1e-6)
    remainder = -damped[...]
    for k in range(8):
        remainder = remainder + left[k] * basis[k * tiles : (k + 1) * tiles, :]
    vector[...] = remainder / length
    lanes = lax.broadcasted_iota(jnp.int32, (1, LANES), 1)
    column = jnp.where(lanes == 8, length, 0.0)
    for k in range(8):
        column = column + jnp.where(lanes == k, coeffs[k], 0.0)
    hessen[...] = column
    keep = lax.broadcasted_iota(jnp.int32, (LANES, LANES), 1) < 96
    for k, v in enumerate(split3(jnp.where(keep, values, 0.0))):
        value_rows[k] = v
    index_rows[...] = second.astype(jnp.int32)
    sub = lax.broadcasted_iota(jnp.int32, (LANES, LANES), 0)
    sub16 = lax.broadcasted_iota(jnp.int32, (16, LANES), 0)
    total = jnp.zeros((48, LANES), F32)
    for s in range(0, LANES, 2):
        left_side, right_side = [], []
        for u in (s, s + 1):
            index = index_rows[u : u + 1, :]
            mask = (index >> 7) == sub16
            left_side.append(
                jnp.concatenate(
                    [jnp.where(mask, value_rows[k, u : u + 1, :], 0.0) for k in range(3)], 0
                ).astype(BF16)
            )
            right_side.append(jnp.where((index & 127) == sub, 1.0, 0.0).astype(BF16))
        total = total + lax.dot_general(
            jnp.concatenate(left_side, 1),
            jnp.concatenate(right_side, 1),
            NT,
            preferred_element_type=F32,
        )
    loads[...] = total[0:16] + total[16:32] + total[32:48]


def shards(
    positions,
    normals,
    patch_extents,
    mirrored_fraction,
    inner_emission_power,
    radiosity,
    basis,
    recv_blocks,
    emit_blocks,
    vis_count,
    owner,
    local_elem,
):
    patches = positions.shape[1]
    tiles = patches // LANES
    n_row, n_col = lax.axis_size("row"), lax.axis_size("col")
    devices = n_row * n_col
    shape = jax.ShapeDtypeStruct

    def rows(array):
        return array.reshape(-1, LANES)

    area = rows(patch_extents)
    basis_rows = rows(basis)
    emit, recv = call(
        functools.partial(stage_kernel, tiles, n_col, n_row),
        (shape((n_col * 9 * tiles, LANES), F32), shape((n_row * 8 * tiles, LANES), F32)),
        in_specs=[VMEM] * 5,
        name="stage",
    )(rows(positions), rows(normals), area, rows(radiosity), basis_rows[7 * tiles :])
    recv = lax.all_to_all(recv.reshape(n_row, -1), "row", 0, 0, tiled=True)
    emit = lax.all_to_all(emit.reshape(n_col, -1), "col", 0, 0, tiled=True)
    owner_rows = rows(owner)
    rank, slots, gram = call(
        functools.partial(rank_kernel, tiles),
        (shape((tiles, LANES), jnp.int32), shape((LANES, LANES), F32), shape((1, LANES), F32)),
        in_specs=[VMEM] * 3,
        name="rank",
    )(owner_rows, rows(local_elem), basis_rows)
    unroll = 16
    part = call(
        functools.partial(pair_kernel, tiles, n_row, n_col, unroll),
        shape((n_row * 2 * tiles, LANES), F32),
        scratch=[
            pltpu.VMEM((n_col * tiles, 64, LANES), BF16),
            pltpu.VMEM((n_row * tiles, 64, 3 * LANES), BF16),
            pltpu.VMEM((64, LANES), BF16),
            pltpu.VMEM((n_row * tiles * 16, LANES), F32),
        ],
        in_specs=[SMEM] * 3 + [VMEM] * 2,
        name="pairs",
    )(vis_count.reshape(-1), recv_blocks.reshape(-1), emit_blocks.reshape(-1), rows(emit), rows(recv))
    part = lax.all_to_all(part.reshape(n_row, -1), "row", 0, 0, tiled=True)
    message, damped = call(
        functools.partial(load_kernel, tiles, n_row),
        (shape((2 * devices, LANES), F32), shape((tiles, LANES), F32)),
        in_specs=[VMEM] * 9,
        name="loads",
    )(
        rows(part),
        basis_rows,
        rows(mirrored_fraction),
        rows(inner_emission_power),
        area,
        owner_rows,
        rank,
        slots,
        gram,
    )
    arrived = lax.all_to_all(message.reshape(devices, -1), ("row", "col"), 0, 0, tiled=True)
    vector, hessen, loads = call(
        functools.partial(finish_kernel, tiles, float(patches * devices)),
        (
            shape((tiles, LANES), F32),
            shape((1, LANES), F32),
            shape((E_DEV // LANES, LANES), F32),
        ),
        scratch=[pltpu.VMEM((3, LANES, LANES), F32), pltpu.VMEM((LANES, LANES), jnp.int32)],
        in_specs=[VMEM] * 3,
        name="finish",
    )(rows(arrived), basis_rows, damped)
    return vector.reshape(-1), hessen.reshape(-1)[:9], loads.reshape(-1)


def solution(mesh):
    in_specs = (
        P(None, ("row", "col")),
        P(None, ("row", "col")),
        P(("row", "col")),
        P(("row", "col")),
        P(("row", "col")),
        P(("row", "col")),
        P(None, ("row", "col")),
        P("row", "col", None),
        P("row", "col", None),
        P("row", "col"),
        P(("row", "col"), None),
        P(("row", "col")),
    )
    out_specs = (P(("row", "col")), P(), P(("row", "col")))
    return jax.shard_map(shards, mesh=mesh, in_specs=in_specs, out_specs=out_specs, check_vma=False)
```

```python
import functools
import math

import jax
import jax.numpy as jnp
from jax import lax
from jax.experimental import pallas as pl
from jax.experimental.pallas import tpu as pltpu
from jax.sharding import Mesh, PartitionSpec as P

F32 = jnp.float32
BF16 = jnp.bfloat16
LANES = 128
AXES = ("pair", "ring", "half", "core")
ROW = ("pair", "ring")
E_DEV = 2048
NT = (((1,), (1,)), ((), ()))
TN = (((0,), (0,)), ((), ()))
VMEM = pl.BlockSpec(memory_space=pltpu.VMEM)
SMEM = pl.BlockSpec(memory_space=pltpu.SMEM)
LIMIT = 32 * 2**20


def split3(value):
    high = value.astype(BF16).astype(F32)
    rest = value - high
    middle = rest.astype(BF16).astype(F32)
    return high, middle, rest - middle


def call(body, out_shape, scratch=(), in_specs=None, name=None, micros=1, limit=LIMIT):
    return pl.pallas_call(
        body,
        out_shape=out_shape,
        in_specs=in_specs,
        out_specs=jax.tree.map(lambda _: VMEM, out_shape),
        scratch_shapes=list(scratch),
        compiler_params=pltpu.CompilerParams(vmem_limit_bytes=limit),
        cost_estimate=pl.CostEstimate(
            flops=int(micros * 1.1e9), bytes_accessed=2**16, transcendentals=0
        ),
        name=name,
    )


def stage_kernel(tiles, copies, pos, nor, area, rad, basis, emit, recv, pos_v, nor_v, area_v, rad_v, last_v, sems):
    moves = [
        pltpu.make_async_copy(source, target, sems.at[k])
        for k, (source, target) in enumerate(
            (
                (pos, pos_v),
                (nor, nor_v),
                (area, area_v),
                (rad, rad_v),
                (basis, last_v),
            )
        )
    ]
    for move in moves:
        move.start()
    for move in moves:
        move.wait()
    x = pos_v[...]
    n = nor_v[...]
    a = area_v[...]
    b = rad_v[...]
    m = (a * b * (1.0 / math.pi)) * n
    product = n * x
    square = x * x
    square = square[0:1] + square[1:2] + square[2:3]
    along = product[0:1] + product[1:2] + product[2:3]
    emit_rows = jnp.concatenate([x, m, square + a, last_v[7:8, :] / b], 0)
    recv_rows = jnp.concatenate([x, n, -along, square], 0)
    for k in range(tiles):
        block = emit_rows[:, k * LANES : (k + 1) * LANES]
        for c in range(copies):
            emit[(c * tiles + k) * 8 : (c * tiles + k + 1) * 8, :] = block
        recv[k * 8 : (k + 1) * 8, :] = recv_rows[:, k * LANES : (k + 1) * LANES]


def rank_kernel(tiles, n_row, n_col, place, owner, elem, basis, recv_list, emit_list, rank, slots, gram, recv_at, emit_at):
    my_pair, my_ring, my_core = place[0], place[1], place[2]
    ring = n_row // 2
    step_of = -(-65536 // tiles)
    r = recv_list[...]
    q = (r * step_of) >> 16
    side = (q >= ring).astype(jnp.int32) ^ my_pair
    recv_at[...] = (((my_ring - q) & (ring - 1)) * 2 + side) * tiles + r - q * tiles
    e = emit_list[...]
    c = (e * step_of) >> 16
    emit_at[...] = ((c >> 1) + ((c ^ my_core) & 1) * (n_col // 2)) * tiles + e - c * tiles
    sub = lax.broadcasted_iota(jnp.int32, (LANES, LANES), 0)
    lane = lax.broadcasted_iota(jnp.int32, (LANES, LANES), 1)
    upper = jnp.concatenate([(sub < lane).astype(BF16), jnp.ones((LANES, LANES), BF16)], 1)
    carry = jnp.zeros((LANES, LANES), F32)
    found = jnp.zeros((LANES, 2 * LANES), F32)
    for g in range(tiles):
        named = owner[g : g + 1, :] == sub
        hot = jnp.where(named, 1.0, 0.0)
        counts = jnp.dot(hot.astype(BF16), upper, preferred_element_type=F32)
        place = jnp.sum(hot * (counts[:, :LANES] + carry), axis=0, keepdims=True)
        carry = carry + counts[:, LANES:]
        place = place.astype(jnp.int32)
        rank[g : g + 1, :] = place
        index = elem[g : g + 1, :]
        high = (index >> 7).astype(F32)
        low = (index & 127).astype(F32)
        at = place == sub
        table = jnp.concatenate([jnp.where(at, high, 0.0), jnp.where(at, low, 0.0)], 0)
        found = found + lax.dot_general(
            hot.astype(BF16), table.astype(BF16), NT, preferred_element_type=F32
        )
    slots[...] = found[:, :LANES] * 128.0 + found[:, LANES:]
    lanes = lax.broadcasted_iota(jnp.int32, (8, LANES), 1)
    subs = lax.broadcasted_iota(jnp.int32, (8, LANES), 0)
    total = jnp.zeros((8, LANES), F32)
    at = 0
    for i in range(8):
        sums = jnp.zeros((8, LANES), F32)
        for g in range(tiles):
            block = basis[:, g * LANES : (g + 1) * LANES]
            sums = sums + block * block[i : i + 1]
        value = jnp.sum(sums, axis=1, keepdims=True)
        total = total + jnp.where((subs >= i) & (lanes == at + subs - i), value, 0.0)
        at += 8 - i
    gram[...] = jnp.sum(total, axis=0, keepdims=True)


def receiver_kernel(*refs):
    wtab = refs[-1]
    row = lax.broadcasted_iota(jnp.int32, (8, LANES), 0)
    zero = jnp.zeros((8, LANES), F32)
    base = 0
    for recv in refs[:-1]:
        blocks = recv.shape[0] // 8

        def body(k, _):
            block = recv[pl.ds(pl.multiple_of(k * 8, 8), 8), :]
            parts = split3(block)
            facing, away, spread = [], [], []
            for p, part in enumerate(parts):
                one = 1.0 if p == 0 else 0.0
                x_low = pltpu.roll(part, 3, 0)
                facing.append(jnp.where(row < 3, pltpu.roll(part, 5, 0), 0.0))
                away.append(jnp.where((row >= 3) & (row < 6), x_low, 0.0))
                spread.append(jnp.where(row < 3, -2.0 * part, jnp.where(row == 6, one, 0.0)))
            consts = []
            for f in (6, 7):
                h, m, l = (part[f : f + 1, :] for part in parts)
                consts.append(
                    jnp.where(row == 0, h, jnp.where(row == 1, m, jnp.where(row == 2, l, 0.0)))
                )
            ones = jnp.where((row >= 3) & (row < 6), 1.0, 0.0)
            for p, (w, c) in enumerate(
                ((facing, consts[0]), (away, ones), (spread, consts[1]))
            ):
                h, m, l = w
                wtab[base + k, :, p * LANES : (p + 1) * LANES] = jnp.concatenate(
                    [h, m, h, l, h, m, c, zero], 0
                ).astype(BF16)
            return 0

        lax.fori_loop(0, blocks, body, 0, unroll=8)
        base += blocks


def pair_kernel(tiles, n_row, n_col, unroll, count, recv_list, emit_list, place, near, far, wtab, out, etab, along, ratio, acc):
    row = lax.broadcasted_iota(jnp.int32, (8, LANES), 0)
    ones3 = jnp.where(row < 3, 1.0, 0.0)
    half = n_col // 2
    blocks = half * tiles
    ratios = []
    for s, source in enumerate((near, far)):
        feature = [source[pl.ds(f, blocks, stride=8), :] for f in range(8)]
        ratios.append(feature[7])
        total = -(feature[0] * feature[3] + feature[1] * feature[4] + feature[2] * feature[5])
        for p, part in enumerate(split3(total)):
            along[p, s * blocks : (s + 1) * blocks, :] = part
    ratios = jnp.concatenate(ratios, 0)
    for k in range(2 * blocks // LANES):
        ratio[k] = ratios[k * LANES : (k + 1) * LANES].T
    for s, source in enumerate((near, far)):

        def body(g, _):
            for k in range(tiles):
                at = g * tiles + k
                h, m, l = split3(source[pl.ds(pl.multiple_of(at * 8, 8), 8), :])
                ph, pm, pl_ = (along[p, pl.ds(s * blocks + at, 1), :] for p in range(3))
                tail = jnp.where(
                    row < 3,
                    1.0,
                    jnp.where(
                        row == 3, ph, jnp.where(row == 4, pm, jnp.where(row == 5, pl_, 0.0))
                    ),
                )
                etab[s * blocks + at] = jnp.concatenate(
                    [h, h, m, h, l, m, tail, jnp.zeros_like(tail)], 0
                ).astype(BF16)
            return 0

        lax.fori_loop(0, half, body, 0)
    acc[...] = jnp.zeros_like(acc)
    live = count[0]

    def fold(full):
        total = full[0:8]
        for k in range(1, LANES // 8):
            total = total + full[8 * k : 8 * k + 8]
        return total

    my_pair, my_ring = place[0], place[1]
    ring = n_row // 2

    def pair(at):
        r = recv_list[at]
        e = emit_list[at]
        g = lax.dot_general(etab[e], wtab[r], TN, preferred_element_type=F32)
        facing = jnp.maximum(g[:, :LANES], 0.0)
        away = jnp.maximum(g[:, LANES : 2 * LANES], 0.0)
        spread = g[:, 2 * LANES :]
        first = facing * away / (spread * spread)
        lane = jnp.full((LANES, LANES), e & (LANES - 1), jnp.int32)
        factor = jnp.take_along_axis(ratio[e >> 7], lane, axis=1, mode="promise_in_bounds")
        return r, fold(first), fold(first * factor)

    def step(i, _):
        found = [pair(i * unroll + k) for k in range(unroll)]
        for k, (r, first, second) in enumerate(found):
            keep = jnp.where(i * unroll + k < live, 1.0, 0.0)
            at = pl.multiple_of(r * 16, 16)
            acc[pl.ds(at, 8), :] = acc[pl.ds(at, 8), :] + first * keep
            acc[pl.ds(at + 8, 8), :] = acc[pl.ds(at + 8, 8), :] + second * keep
        return 0

    lax.fori_loop(0, (live + unroll - 1) // unroll, step, 0)
    for q in range(n_row):
        target = (my_pair ^ (q & 1)) * ring + ((my_ring - (q >> 1)) & (ring - 1))
        for v in range(2):
            total = acc[pl.ds(q * tiles * 16 + v * 8, tiles, stride=16), :]
            for s in range(1, 8):
                total = total + acc[pl.ds(q * tiles * 16 + v * 8 + s, tiles, stride=16), :]
            at = pl.multiple_of((target * 2 + v) * tiles, 8)
            out[pl.ds(at, tiles), :] = total


def load_kernel(tiles, n_row, part, basis, mirrored, inner, area, owner, rank, slots, gram, message, damped):
    sub = lax.broadcasted_iota(jnp.int32, (LANES, LANES), 0)
    irradiance = part[0:tiles, :]
    scattered = part[tiles : 2 * tiles, :]
    for q in range(1, n_row):
        irradiance = irradiance + part[2 * q * tiles : (2 * q + 1) * tiles, :]
        scattered = scattered + part[(2 * q + 1) * tiles : (2 * q + 2) * tiles, :]
    fraction = mirrored[...]
    lost = fraction * scattered
    damped[...] = lost
    power = (1.0 - fraction) * irradiance + inner[...]
    load = 20.0 * area[...] * jnp.sqrt(jnp.sqrt(power))
    parts = split3(load)
    found = jnp.zeros((LANES, LANES), F32)
    for g in range(tiles):
        hot = jnp.where(owner[g : g + 1, :] == sub, 1.0, 0.0).astype(BF16)
        at = rank[g : g + 1, :] == sub
        table = jnp.concatenate([jnp.where(at, v[g : g + 1, :], 0.0) for v in parts], 1)
        found = found + lax.dot_general(
            jnp.concatenate([hot] * 3, 1), table.astype(BF16), NT, preferred_element_type=F32
        )
    lanes = lax.broadcasted_iota(jnp.int32, (8, LANES), 1)
    subs = lax.broadcasted_iota(jnp.int32, (8, LANES), 0)
    sums = jnp.zeros((8, LANES), F32)
    for g in range(tiles):
        sums = sums + basis[:, g * LANES : (g + 1) * LANES] * lost[g : g + 1, :]
    inner_products = jnp.sum(sums, axis=1, keepdims=True)
    square = jnp.sum(lost * lost, axis=(0, 1), keepdims=True)
    stats = jnp.sum(
        jnp.where(lanes == 96 + subs, inner_products, 0.0), axis=0, keepdims=True
    )
    g = jnp.broadcast_to(gram[...], (8, LANES))
    lane = lanes[0:1]
    stats = jnp.where(lane == 104, square, stats)
    stats = jnp.where(lane >= 105, pltpu.roll(g, 105, 1)[0:1], stats)
    more = pltpu.roll(g, 73, 1)[0:1]
    keep = lax.broadcasted_iota(jnp.int32, (LANES, LANES), 1) < 96
    message[pl.ds(0, LANES, stride=2), :] = jnp.where(keep, found, stats)
    message[pl.ds(1, LANES, stride=2), :] = jnp.where(keep, slots[...], more)


def finish_kernel(tiles, cells, arrived, basis, damped, vector, hessen, loads, value_rows, index_rows):
    values = arrived[pl.ds(0, LANES, stride=2), :]
    second = arrived[pl.ds(1, LANES, stride=2), :]
    top = jnp.sum(values, axis=0, keepdims=True)
    low = jnp.sum(second, axis=0, keepdims=True)
    inner = [top[:, 96 + k : 97 + k] for k in range(8)]
    lost_square = top[:, 104:105]
    gram = {}
    at = 0
    for i in range(8):
        for j in range(i, 8):
            lane = 105 + at
            gram[i, j] = top[:, lane : lane + 1] if lane < 128 else low[:, lane - 32 : lane - 31]
            gram[j, i] = gram[i, j]
            at += 1
    scale = 1.0 / cells
    coeffs = [(gram[7, k] - inner[k]) * scale for k in range(8)]
    left = [(1.0 if k == 7 else 0.0) - coeffs[k] for k in range(8)]
    square = lost_square
    for i in range(8):
        line = gram[i, i] * left[i] - 2.0 * inner[i]
        for j in range(i + 1, 8):
            line = line + 2.0 * gram[i, j] * left[j]
        square = square + line * left[i]
    length = jnp.sqrt(jnp.maximum(square, 0.0) * scale + 1e-6)
    subs = lax.broadcasted_iota(jnp.int32, (8, LANES), 0)
    weights = jnp.zeros((8, LANES), F32)
    for k in range(8):
        weights = jnp.where(subs == k, left[k], weights)
    for g in range(tiles):
        mixed = jnp.sum(basis[:, g * LANES : (g + 1) * LANES] * weights, axis=0, keepdims=True)
        vector[g : g + 1, :] = (mixed - damped[g : g + 1, :]) / length
    lanes = lax.broadcasted_iota(jnp.int32, (1, LANES), 1)
    column = jnp.where(lanes == 8, length, 0.0)
    for k in range(8):
        column = jnp.where(lanes == k, coeffs[k], column)
    hessen[...] = column[:, 0:9]
    keep = lax.broadcasted_iota(jnp.int32, (LANES, LANES), 1) < 96
    for k, v in enumerate(split3(jnp.where(keep, values, 0.0))):
        value_rows[k] = v
    index_rows[...] = second.astype(jnp.int32)
    sub = lax.broadcasted_iota(jnp.int32, (LANES, LANES), 0)
    sub16 = lax.broadcasted_iota(jnp.int32, (16, LANES), 0)
    total = jnp.zeros((48, LANES), F32)
    for s in range(0, LANES, 2):
        left_side, right_side = [], []
        for u in (s, s + 1):
            index = index_rows[u : u + 1, :]
            mask = (index >> 7) == sub16
            left_side.append(
                jnp.concatenate(
                    [jnp.where(mask, value_rows[k, u : u + 1, :], 0.0) for k in range(3)], 0
                ).astype(BF16)
            )
            right_side.append(jnp.where((index & 127) == sub, 1.0, 0.0).astype(BF16))
        total = total + lax.dot_general(
            jnp.concatenate(left_side, 1),
            jnp.concatenate(right_side, 1),
            NT,
            preferred_element_type=F32,
        )
    loads[...] = total[0:16] + total[16:32] + total[32:48]


def shards(
    positions,
    normals,
    patch_extents,
    mirrored_fraction,
    inner_emission_power,
    radiosity,
    basis,
    recv_blocks,
    emit_blocks,
    vis_count,
    owner,
    local_elem,
):
    patches = positions.shape[1]
    tiles = patches // LANES
    pairs_of, ring, half, cores = (lax.axis_size(a) for a in AXES)
    n_row, n_col = pairs_of * ring, half * cores
    devices = n_row * n_col
    place = jnp.stack([lax.axis_index(a) for a in ("pair", "ring", "core")])
    shape = jax.ShapeDtypeStruct

    def rows(array):
        return array.reshape(-1, LANES)

    emit, recv = call(
        functools.partial(stage_kernel, tiles, half),
        (shape((half * 8 * tiles, LANES), F32), shape((8 * tiles, LANES), F32)),
        scratch=[
            pltpu.VMEM((3, patches), F32),
            pltpu.VMEM((3, patches), F32),
            pltpu.VMEM((1, patches), F32),
            pltpu.VMEM((1, patches), F32),
            pltpu.VMEM((8, patches), F32),
            pltpu.SemaphoreType.DMA((5,)),
        ],
        in_specs=[pl.BlockSpec(memory_space=pl.ANY)] * 5,
        name="stage",
        limit=60 * 2**20,
    )(positions, normals, patch_extents[None], radiosity[None], basis)
    swapped = lax.ppermute(recv, "pair", [(0, 1), (1, 0)])
    emit, swapped = lax.optimization_barrier((emit, swapped))
    both = jnp.concatenate([recv, swapped], 0)
    owner_rows, both_again = lax.optimization_barrier((rows(owner), both))
    lists = rows(recv_blocks), rows(emit_blocks)
    rank, slots, gram, recv_at, emit_at = call(
        functools.partial(rank_kernel, tiles, n_row, n_col),
        (
            shape((tiles, LANES), jnp.int32),
            shape((LANES, LANES), F32),
            shape((1, LANES), F32),
            shape(lists[0].shape, jnp.int32),
            shape(lists[1].shape, jnp.int32),
        ),
        in_specs=[SMEM] + [VMEM] * 5,
        name="rank",
        micros=20,
        limit=60 * 2**20,
    )(place, owner_rows, rows(local_elem), basis, *lists)
    received = [both_again] + [
        lax.ppermute(both, "ring", [(i, (i + k) % ring) for i in range(ring)])
        for k in range(1, ring)
    ]
    near = rows(lax.all_to_all(emit.reshape(half, -1), "half", 0, 0, tiled=True))
    near, received, recv_at, emit_at = lax.optimization_barrier(
        (near, received, recv_at, emit_at)
    )
    far = lax.ppermute(near, "core", [(0, 1), (1, 0)])
    wtab = call(
        receiver_kernel,
        shape((n_row * tiles, 64, 3 * LANES), BF16),
        in_specs=[VMEM] * len(received),
        name="receivers",
        micros=4,
    )(*received)
    unroll = 32
    part = call(
        functools.partial(pair_kernel, tiles, n_row, n_col, unroll),
        shape((n_row * 2 * tiles, LANES), F32),
        scratch=[
            pltpu.VMEM((n_col * tiles, 64, LANES), BF16),
            pltpu.VMEM((3, n_col * tiles, LANES), F32),
            pltpu.VMEM((n_col * tiles // LANES, LANES, LANES), F32),
            pltpu.VMEM((n_row * tiles * 16, LANES), F32),
        ],
        in_specs=[SMEM] * 4 + [VMEM] * 3,
        name="pairs",
        micros=20,
    )(
        vis_count.reshape(-1),
        recv_at.reshape(-1),
        emit_at.reshape(-1),
        place,
        near,
        far,
        wtab,
    )
    part = lax.all_to_all(part.reshape(n_row, -1), ROW, 0, 0, tiled=True)
    message, damped = call(
        functools.partial(load_kernel, tiles, n_row),
        (shape((2 * devices, LANES), F32), shape((tiles, LANES), F32)),
        in_specs=[VMEM] * 9,
        name="loads",
    )(
        rows(part),
        basis,
        rows(mirrored_fraction),
        rows(inner_emission_power),
        rows(patch_extents),
        owner_rows,
        rank,
        slots,
        gram,
    )
    arrived = lax.all_to_all(message.reshape(devices, -1), AXES, 0, 0, tiled=True)
    vector, hessen, loads = call(
        functools.partial(finish_kernel, tiles, float(patches * devices)),
        (
            shape((tiles, LANES), F32),
            shape((1, 9), F32),
            shape((E_DEV // LANES, LANES), F32),
        ),
        scratch=[pltpu.VMEM((3, LANES, LANES), F32), pltpu.VMEM((LANES, LANES), jnp.int32)],
        in_specs=[VMEM] * 3,
        name="finish",
    )(rows(arrived), basis, damped)
    return vector.reshape(-1), hessen.reshape(-1), loads.reshape(-1)


def solution(mesh):
    n_row, n_col = mesh.shape["row"], mesh.shape["col"]
    fine = Mesh(mesh.devices.reshape(2, n_row // 2, n_col // 2, 2), AXES)
    every = P(AXES)
    second = P(None, AXES)
    grid = P(ROW, ("half", "core"))
    in_specs = (
        second,
        second,
        every,
        every,
        every,
        every,
        second,
        P(ROW, ("half", "core"), None),
        P(ROW, ("half", "core"), None),
        grid,
        P(AXES, None),
        every,
    )
    return jax.shard_map(
        shards, mesh=fine, in_specs=in_specs, out_specs=(every, P(), every), check_vma=False
    )
```

```python
import functools
import math

import jax
import jax.numpy as jnp
from jax import lax
from jax.experimental import pallas as pl
from jax.experimental.pallas import tpu as pltpu
from jax.sharding import Mesh, PartitionSpec as P

F32 = jnp.float32
BF16 = jnp.bfloat16
LANES = 128
AXES = ("pair", "ring", "half", "core")
ROW = ("pair", "ring")
E_DEV = 2048
NT = (((1,), (1,)), ((), ()))
TN = (((0,), (0,)), ((), ()))
VMEM = pl.BlockSpec(memory_space=pltpu.VMEM)
SMEM = pl.BlockSpec(memory_space=pltpu.SMEM)
LIMIT = 32 * 2**20


def split3(value):
    high = value.astype(BF16).astype(F32)
    rest = value - high
    middle = rest.astype(BF16).astype(F32)
    return high, middle, rest - middle


def call(body, out_shape, scratch=(), in_specs=None, name=None, micros=1, limit=LIMIT):
    return pl.pallas_call(
        body,
        out_shape=out_shape,
        in_specs=in_specs,
        out_specs=jax.tree.map(lambda _: VMEM, out_shape),
        scratch_shapes=list(scratch),
        compiler_params=pltpu.CompilerParams(vmem_limit_bytes=limit),
        cost_estimate=pl.CostEstimate(
            flops=int(micros * 1.1e9), bytes_accessed=2**16, transcendentals=0
        ),
        name=name,
    )


def fetch(sources, targets, sems):
    moves = [
        pltpu.make_async_copy(source, target, sems.at[k])
        for k, (source, target) in enumerate(zip(sources, targets))
    ]
    for move in moves:
        move.start()
    for move in moves:
        move.wait()


def emit_kernel(tiles, copies, pos, nor, area, rad, basis, emit, pos_v, nor_v, area_v, rad_v, basis_v, sems):
    fetch((pos, nor, area, rad, basis), (pos_v, nor_v, area_v, rad_v, basis_v), sems)
    x = pos_v[...]
    n = nor_v[...]
    a = area_v[...]
    b = rad_v[...]
    m = (a * b * (1.0 / math.pi)) * n
    square = x * x
    square = square[0:1] + square[1:2] + square[2:3]
    emit_rows = jnp.concatenate([x, m, square + a, basis_v[7:8, :] / b], 0)
    for k in range(tiles):
        block = emit_rows[:, k * LANES : (k + 1) * LANES]
        for c in range(copies):
            emit[(c * tiles + k) * 8 : (c * tiles + k + 1) * 8, :] = block


def join_kernel(tiles, own_pos, own_nor, pos, nor, both):
    base = 0
    for x_ref, n_ref in ((own_pos, own_nor), (pos, nor)):
        x = x_ref[...]
        n = n_ref[...]
        product = n * x
        square = x * x
        square = square[0:1] + square[1:2] + square[2:3]
        along = product[0:1] + product[1:2] + product[2:3]
        rows = jnp.concatenate([x, n, -along, square], 0)
        for k in range(tiles):
            both[base + k * 8 : base + (k + 1) * 8, :] = rows[:, k * LANES : (k + 1) * LANES]
        base += tiles * 8


def rank_kernel(tiles, n_row, n_col, place, owner, elem, basis, recv_list, emit_list, rank, slots, gram, recv_at, emit_at):
    my_pair, my_ring, my_core = place[0], place[1], place[2]
    ring = n_row // 2
    step_of = -(-65536 // tiles)
    r = recv_list[...]
    q = (r * step_of) >> 16
    side = (q >= ring).astype(jnp.int32) ^ my_pair
    recv_at[...] = (((my_ring - q) & (ring - 1)) * 2 + side) * tiles + r - q * tiles
    e = emit_list[...]
    c = (e * step_of) >> 16
    emit_at[...] = ((c >> 1) + ((c ^ my_core) & 1) * (n_col // 2)) * tiles + e - c * tiles
    sub = lax.broadcasted_iota(jnp.int32, (LANES, LANES), 0)
    lane = lax.broadcasted_iota(jnp.int32, (LANES, LANES), 1)
    upper = jnp.concatenate([(sub < lane).astype(BF16), jnp.ones((LANES, LANES), BF16)], 1)
    carry = jnp.zeros((LANES, LANES), F32)
    found = jnp.zeros((LANES, 2 * LANES), F32)
    for g in range(tiles):
        named = owner[g : g + 1, :] == sub
        hot = jnp.where(named, 1.0, 0.0)
        counts = jnp.dot(hot.astype(BF16), upper, preferred_element_type=F32)
        place = jnp.sum(hot * (counts[:, :LANES] + carry), axis=0, keepdims=True)
        carry = carry + counts[:, LANES:]
        place = place.astype(jnp.int32)
        rank[g : g + 1, :] = place
        index = elem[g : g + 1, :]
        high = (index >> 7).astype(F32)
        low = (index & 127).astype(F32)
        at = place == sub
        table = jnp.concatenate([jnp.where(at, high, 0.0), jnp.where(at, low, 0.0)], 0)
        found = found + lax.dot_general(
            hot.astype(BF16), table.astype(BF16), NT, preferred_element_type=F32
        )
    slots[...] = found[:, :LANES] * 128.0 + found[:, LANES:]
    lanes = lax.broadcasted_iota(jnp.int32, (8, LANES), 1)
    subs = lax.broadcasted_iota(jnp.int32, (8, LANES), 0)
    total = jnp.zeros((8, LANES), F32)
    at = 0
    for i in range(8):
        sums = jnp.zeros((8, LANES), F32)
        for g in range(tiles):
            block = basis[:, g * LANES : (g + 1) * LANES]
            sums = sums + block * block[i : i + 1]
        value = jnp.sum(sums, axis=1, keepdims=True)
        total = total + jnp.where((subs >= i) & (lanes == at + subs - i), value, 0.0)
        at += 8 - i
    gram[...] = jnp.sum(total, axis=0, keepdims=True)


def receiver_kernel(*refs):
    wtab = refs[-1]
    row = lax.broadcasted_iota(jnp.int32, (8, LANES), 0)
    zero = jnp.zeros((8, LANES), F32)
    base = 0
    for recv in refs[:-1]:
        blocks = recv.shape[0] // 8

        def body(k, _):
            block = recv[pl.ds(pl.multiple_of(k * 8, 8), 8), :]
            parts = split3(block)
            facing, away, spread = [], [], []
            for p, part in enumerate(parts):
                one = 1.0 if p == 0 else 0.0
                x_low = pltpu.roll(part, 3, 0)
                facing.append(jnp.where(row < 3, pltpu.roll(part, 5, 0), 0.0))
                away.append(jnp.where((row >= 3) & (row < 6), x_low, 0.0))
                spread.append(jnp.where(row < 3, -2.0 * part, jnp.where(row == 6, one, 0.0)))
            consts = []
            for f in (6, 7):
                h, m, l = (part[f : f + 1, :] for part in parts)
                consts.append(
                    jnp.where(row == 0, h, jnp.where(row == 1, m, jnp.where(row == 2, l, 0.0)))
                )
            ones = jnp.where((row >= 3) & (row < 6), 1.0, 0.0)
            for p, (w, c) in enumerate(
                ((facing, consts[0]), (away, ones), (spread, consts[1]))
            ):
                h, m, l = w
                wtab[base + k, :, p * LANES : (p + 1) * LANES] = jnp.concatenate(
                    [h, m, h, l, h, m, c, zero], 0
                ).astype(BF16)
            return 0

        lax.fori_loop(0, blocks, body, 0, unroll=8)
        base += blocks


def pair_kernel(tiles, n_row, n_col, unroll, count, recv_list, emit_list, place, near, far, wtab, out, etab, along, ratio, acc):
    row = lax.broadcasted_iota(jnp.int32, (8, LANES), 0)
    ones3 = jnp.where(row < 3, 1.0, 0.0)
    half = n_col // 2
    blocks = half * tiles
    ratios = []
    for s, source in enumerate((near, far)):
        feature = [source[pl.ds(f, blocks, stride=8), :] for f in range(8)]
        ratios.append(feature[7])
        total = -(feature[0] * feature[3] + feature[1] * feature[4] + feature[2] * feature[5])
        for p, part in enumerate(split3(total)):
            along[p, s * blocks : (s + 1) * blocks, :] = part
    ratios = jnp.concatenate(ratios, 0)
    for k in range(2 * blocks // LANES):
        ratio[k] = ratios[k * LANES : (k + 1) * LANES].T
    for s, source in enumerate((near, far)):

        def body(g, _):
            for k in range(tiles):
                at = g * tiles + k
                h, m, l = split3(source[pl.ds(pl.multiple_of(at * 8, 8), 8), :])
                ph, pm, pl_ = (along[p, pl.ds(s * blocks + at, 1), :] for p in range(3))
                tail = jnp.where(
                    row < 3,
                    1.0,
                    jnp.where(
                        row == 3, ph, jnp.where(row == 4, pm, jnp.where(row == 5, pl_, 0.0))
                    ),
                )
                etab[s * blocks + at] = jnp.concatenate(
                    [h, h, m, h, l, m, tail, jnp.zeros_like(tail)], 0
                ).astype(BF16)
            return 0

        lax.fori_loop(0, half, body, 0)
    acc[...] = jnp.zeros_like(acc)
    live = count[0]

    def fold(full):
        total = full[0:8]
        for k in range(1, LANES // 8):
            total = total + full[8 * k : 8 * k + 8]
        return total

    my_pair, my_ring = place[0], place[1]
    ring = n_row // 2

    empty = jnp.zeros((64, 3 * LANES), BF16)

    def view(g, e):
        facing = jnp.maximum(g[:, :LANES], 0.0)
        away = jnp.maximum(g[:, LANES : 2 * LANES], 0.0)
        spread = g[:, 2 * LANES :]
        first = facing * away / (spread * spread)
        lane = jnp.full((LANES, LANES), e & (LANES - 1), jnp.int32)
        factor = jnp.take_along_axis(ratio[e >> 7], lane, axis=1, mode="promise_in_bounds")
        return fold(first), fold(first * factor)

    def two(at):
        r = recv_list[at], recv_list[at + 1]
        e = emit_list[at], emit_list[at + 1]
        weights = jnp.concatenate(
            [
                jnp.concatenate([wtab[r[0]], empty], 0),
                jnp.concatenate([empty, wtab[r[1]]], 0),
            ],
            1,
        )
        g = lax.dot_general(
            jnp.concatenate([etab[e[0]], etab[e[1]]], 0), weights, TN, preferred_element_type=F32
        )
        return [
            (r[k],) + view(g[:, 3 * k * LANES : 3 * (k + 1) * LANES], e[k]) for k in range(2)
        ]

    def step(i, _):
        found = []
        for k in range(0, unroll, 2):
            found += two(i * unroll + k)
        for k, (r, first, second) in enumerate(found):
            keep = jnp.where(i * unroll + k < live, 1.0, 0.0)
            at = pl.multiple_of(r * 16, 16)
            acc[pl.ds(at, 8), :] = acc[pl.ds(at, 8), :] + first * keep
            acc[pl.ds(at + 8, 8), :] = acc[pl.ds(at + 8, 8), :] + second * keep
        return 0

    lax.fori_loop(0, (live + unroll - 1) // unroll, step, 0)
    for q in range(n_row):
        target = (my_pair ^ (q & 1)) * ring + ((my_ring - (q >> 1)) & (ring - 1))
        for v in range(2):
            total = acc[pl.ds(q * tiles * 16 + v * 8, tiles, stride=16), :]
            for s in range(1, 8):
                total = total + acc[pl.ds(q * tiles * 16 + v * 8 + s, tiles, stride=16), :]
            at = pl.multiple_of((target * 2 + v) * tiles, 8)
            out[pl.ds(at, tiles), :] = total


def load_kernel(tiles, n_row, part, basis, mirrored, inner, area, owner, rank, slots, gram, message, damped):
    sub = lax.broadcasted_iota(jnp.int32, (LANES, LANES), 0)
    irradiance = part[0:tiles, :]
    scattered = part[tiles : 2 * tiles, :]
    for q in range(1, n_row):
        irradiance = irradiance + part[2 * q * tiles : (2 * q + 1) * tiles, :]
        scattered = scattered + part[(2 * q + 1) * tiles : (2 * q + 2) * tiles, :]
    fraction = mirrored[...]
    lost = fraction * scattered
    damped[...] = lost
    power = (1.0 - fraction) * irradiance + inner[...]
    load = 20.0 * area[...] * jnp.sqrt(jnp.sqrt(power))
    parts = split3(load)
    found = jnp.zeros((LANES, LANES), F32)
    for g in range(tiles):
        hot = jnp.where(owner[g : g + 1, :] == sub, 1.0, 0.0).astype(BF16)
        at = rank[g : g + 1, :] == sub
        table = jnp.concatenate([jnp.where(at, v[g : g + 1, :], 0.0) for v in parts], 1)
        found = found + lax.dot_general(
            jnp.concatenate([hot] * 3, 1), table.astype(BF16), NT, preferred_element_type=F32
        )
    lanes = lax.broadcasted_iota(jnp.int32, (8, LANES), 1)
    subs = lax.broadcasted_iota(jnp.int32, (8, LANES), 0)
    sums = jnp.zeros((8, LANES), F32)
    for g in range(tiles):
        sums = sums + basis[:, g * LANES : (g + 1) * LANES] * lost[g : g + 1, :]
    inner_products = jnp.sum(sums, axis=1, keepdims=True)
    square = jnp.sum(lost * lost, axis=(0, 1), keepdims=True)
    stats = jnp.sum(
        jnp.where(lanes == 96 + subs, inner_products, 0.0), axis=0, keepdims=True
    )
    g = jnp.broadcast_to(gram[...], (8, LANES))
    lane = lanes[0:1]
    stats = jnp.where(lane == 104, square, stats)
    stats = jnp.where(lane >= 105, pltpu.roll(g, 105, 1)[0:1], stats)
    more = pltpu.roll(g, 73, 1)[0:1]
    keep = lax.broadcasted_iota(jnp.int32, (LANES, LANES), 1) < 96
    message[pl.ds(0, LANES, stride=2), :] = jnp.where(keep, found, stats)
    message[pl.ds(1, LANES, stride=2), :] = jnp.where(keep, slots[...], more)


def finish_kernel(tiles, cells, arrived, basis, damped, vector, hessen, loads, value_rows, index_rows):
    values = arrived[pl.ds(0, LANES, stride=2), :]
    second = arrived[pl.ds(1, LANES, stride=2), :]
    top = jnp.sum(values, axis=0, keepdims=True)
    low = jnp.sum(second, axis=0, keepdims=True)
    inner = [top[:, 96 + k : 97 + k] for k in range(8)]
    lost_square = top[:, 104:105]
    gram = {}
    at = 0
    for i in range(8):
        for j in range(i, 8):
            lane = 105 + at
            gram[i, j] = top[:, lane : lane + 1] if lane < 128 else low[:, lane - 32 : lane - 31]
            gram[j, i] = gram[i, j]
            at += 1
    scale = 1.0 / cells
    coeffs = [(gram[7, k] - inner[k]) * scale for k in range(8)]
    left = [(1.0 if k == 7 else 0.0) - coeffs[k] for k in range(8)]
    square = lost_square
    for i in range(8):
        line = gram[i, i] * left[i] - 2.0 * inner[i]
        for j in range(i + 1, 8):
            line = line + 2.0 * gram[i, j] * left[j]
        square = square + line * left[i]
    length = jnp.sqrt(jnp.maximum(square, 0.0) * scale + 1e-6)
    subs = lax.broadcasted_iota(jnp.int32, (8, LANES), 0)
    weights = jnp.zeros((8, LANES), F32)
    for k in range(8):
        weights = jnp.where(subs == k, left[k], weights)
    for g in range(tiles):
        mixed = jnp.sum(basis[:, g * LANES : (g + 1) * LANES] * weights, axis=0, keepdims=True)
        vector[g : g + 1, :] = (mixed - damped[g : g + 1, :]) / length
    lanes = lax.broadcasted_iota(jnp.int32, (1, LANES), 1)
    column = jnp.where(lanes == 8, length, 0.0)
    for k in range(8):
        column = jnp.where(lanes == k, coeffs[k], column)
    hessen[...] = column[:, 0:9]
    keep = lax.broadcasted_iota(jnp.int32, (LANES, LANES), 1) < 96
    for k, v in enumerate(split3(jnp.where(keep, values, 0.0))):
        value_rows[k] = v
    index_rows[...] = second.astype(jnp.int32)
    sub = lax.broadcasted_iota(jnp.int32, (LANES, LANES), 0)
    sub16 = lax.broadcasted_iota(jnp.int32, (16, LANES), 0)
    total = jnp.zeros((48, LANES), F32)
    for s in range(0, LANES, 2):
        left_side, right_side = [], []
        for u in (s, s + 1):
            index = index_rows[u : u + 1, :]
            mask = (index >> 7) == sub16
            left_side.append(
                jnp.concatenate(
                    [jnp.where(mask, value_rows[k, u : u + 1, :], 0.0) for k in range(3)], 0
                ).astype(BF16)
            )
            right_side.append(jnp.where((index & 127) == sub, 1.0, 0.0).astype(BF16))
        total = total + lax.dot_general(
            jnp.concatenate(left_side, 1),
            jnp.concatenate(right_side, 1),
            NT,
            preferred_element_type=F32,
        )
    loads[...] = total[0:16] + total[16:32] + total[32:48]


def shards(
    positions,
    normals,
    patch_extents,
    mirrored_fraction,
    inner_emission_power,
    radiosity,
    basis,
    recv_blocks,
    emit_blocks,
    vis_count,
    owner,
    local_elem,
):
    patches = positions.shape[1]
    tiles = patches // LANES
    pairs_of, ring, half, cores = (lax.axis_size(a) for a in AXES)
    n_row, n_col = pairs_of * ring, half * cores
    devices = n_row * n_col
    place = jnp.stack([lax.axis_index(a) for a in ("pair", "ring", "core")])
    shape = jax.ShapeDtypeStruct

    def rows(array):
        return array.reshape(-1, LANES)

    hbm = pl.BlockSpec(memory_space=pl.ANY)
    swap = [(0, 1), (1, 0)]
    swapped = [lax.ppermute(array, "pair", swap) for array in (positions, normals)]
    emit = call(
        functools.partial(emit_kernel, tiles, half),
        shape((half * 8 * tiles, LANES), F32),
        scratch=[
            pltpu.VMEM((3, patches), F32),
            pltpu.VMEM((3, patches), F32),
            pltpu.VMEM((1, patches), F32),
            pltpu.VMEM((1, patches), F32),
            pltpu.VMEM((8, patches), F32),
            pltpu.SemaphoreType.DMA((5,)),
        ],
        in_specs=[hbm] * 5,
        name="emit",
        micros=4,
        limit=60 * 2**20,
    )(positions, normals, patch_extents[None], radiosity[None], basis)
    both = call(
        functools.partial(join_kernel, tiles),
        shape((16 * tiles, LANES), F32),
        in_specs=[VMEM] * 4,
        name="join",
        micros=3,
    )(positions, normals, *swapped)
    owner_rows, both_again = lax.optimization_barrier((rows(owner), both))
    lists = rows(recv_blocks), rows(emit_blocks)
    rank, slots, gram, recv_at, emit_at = call(
        functools.partial(rank_kernel, tiles, n_row, n_col),
        (
            shape((tiles, LANES), jnp.int32),
            shape((LANES, LANES), F32),
            shape((1, LANES), F32),
            shape(lists[0].shape, jnp.int32),
            shape(lists[1].shape, jnp.int32),
        ),
        in_specs=[SMEM] + [VMEM] * 5,
        name="rank",
        micros=3,
        limit=60 * 2**20,
    )(place, owner_rows, rows(local_elem), basis, *lists)
    received = [both_again] + [
        lax.ppermute(both, "ring", [(i, (i + k) % ring) for i in range(ring)])
        for k in range(1, ring)
    ]
    near = rows(lax.all_to_all(emit.reshape(half, -1), "half", 0, 0, tiled=True))
    near, received, recv_at, emit_at = lax.optimization_barrier(
        (near, received, recv_at, emit_at)
    )
    far = lax.ppermute(near, "core", [(0, 1), (1, 0)])
    wtab = call(
        receiver_kernel,
        shape((n_row * tiles, 64, 3 * LANES), BF16),
        in_specs=[VMEM] * len(received),
        name="receivers",
        micros=4,
    )(*received)
    unroll = 64
    part = call(
        functools.partial(pair_kernel, tiles, n_row, n_col, unroll),
        shape((n_row * 2 * tiles, LANES), F32),
        scratch=[
            pltpu.VMEM((n_col * tiles, 64, LANES), BF16),
            pltpu.VMEM((3, n_col * tiles, LANES), F32),
            pltpu.VMEM((n_col * tiles // LANES, LANES, LANES), F32),
            pltpu.VMEM((n_row * tiles * 16, LANES), F32),
        ],
        in_specs=[SMEM] * 4 + [VMEM] * 3,
        name="pairs",
        micros=20,
    )(
        vis_count.reshape(-1),
        recv_at.reshape(-1),
        emit_at.reshape(-1),
        place,
        near,
        far,
        wtab,
    )
    part = lax.all_to_all(part.reshape(n_row, -1), ROW, 0, 0, tiled=True)
    message, damped = call(
        functools.partial(load_kernel, tiles, n_row),
        (shape((2 * devices, LANES), F32), shape((tiles, LANES), F32)),
        in_specs=[VMEM] * 9,
        name="loads",
    )(
        rows(part),
        basis,
        rows(mirrored_fraction),
        rows(inner_emission_power),
        rows(patch_extents),
        owner_rows,
        rank,
        slots,
        gram,
    )
    arrived = lax.all_to_all(message.reshape(devices, -1), AXES, 0, 0, tiled=True)
    vector, hessen, loads = call(
        functools.partial(finish_kernel, tiles, float(patches * devices)),
        (
            shape((tiles, LANES), F32),
            shape((1, 9), F32),
            shape((E_DEV // LANES, LANES), F32),
        ),
        scratch=[pltpu.VMEM((3, LANES, LANES), F32), pltpu.VMEM((LANES, LANES), jnp.int32)],
        in_specs=[VMEM] * 3,
        name="finish",
    )(rows(arrived), basis, damped)
    return vector.reshape(-1), hessen.reshape(-1), loads.reshape(-1)


def solution(mesh):
    n_row, n_col = mesh.shape["row"], mesh.shape["col"]
    fine = Mesh(mesh.devices.reshape(2, n_row // 2, n_col // 2, 2), AXES)
    every = P(AXES)
    second = P(None, AXES)
    grid = P(ROW, ("half", "core"))
    in_specs = (
        second,
        second,
        every,
        every,
        every,
        every,
        second,
        P(ROW, ("half", "core"), None),
        P(ROW, ("half", "core"), None),
        grid,
        P(AXES, None),
        every,
    )
    return jax.shard_map(
        shards, mesh=fine, in_specs=in_specs, out_specs=(every, P(), every), check_vma=False
    )
```

```python
import functools
import math

import jax
import jax.numpy as jnp
from jax import lax
from jax.experimental import pallas as pl
from jax.experimental.pallas import tpu as pltpu
from jax.sharding import Mesh, PartitionSpec as P

F32 = jnp.float32
BF16 = jnp.bfloat16
LANES = 128
AXES = ("pair", "ring", "half", "core")
ROW = ("pair", "ring")
E_DEV = 2048
NT = (((1,), (1,)), ((), ()))
TN = (((0,), (0,)), ((), ()))
VMEM = pl.BlockSpec(memory_space=pltpu.VMEM)
SMEM = pl.BlockSpec(memory_space=pltpu.SMEM)
LIMIT = 32 * 2**20


def split3(value):
    high = value.astype(BF16).astype(F32)
    rest = value - high
    middle = rest.astype(BF16).astype(F32)
    return high, middle, rest - middle


def call(body, out_shape, scratch=(), in_specs=None, name=None, micros=1, limit=LIMIT):
    return pl.pallas_call(
        body,
        out_shape=out_shape,
        in_specs=in_specs,
        out_specs=jax.tree.map(lambda _: VMEM, out_shape),
        scratch_shapes=list(scratch),
        compiler_params=pltpu.CompilerParams(vmem_limit_bytes=limit),
        cost_estimate=pl.CostEstimate(
            flops=int(micros * 1.1e9), bytes_accessed=2**16, transcendentals=0
        ),
        name=name,
    )


def fetch(sources, targets, sems):
    moves = [
        pltpu.make_async_copy(source, target, sems.at[k])
        for k, (source, target) in enumerate(zip(sources, targets))
    ]
    for move in moves:
        move.start()
    for move in moves:
        move.wait()


def emit_kernel(tiles, copies, pos, nor, area, rad, basis, emit, pos_v, nor_v, area_v, rad_v, basis_v, sems):
    fetch((pos, nor, area, rad, basis), (pos_v, nor_v, area_v, rad_v, basis_v), sems)
    x = pos_v[...]
    n = nor_v[...]
    a = area_v[...]
    b = rad_v[...]
    m = (a * b * (1.0 / math.pi)) * n
    square = x * x
    square = square[0:1] + square[1:2] + square[2:3]
    emit_rows = jnp.concatenate([x, m, square + a, basis_v[7:8, :] / b], 0)
    for k in range(tiles):
        block = emit_rows[:, k * LANES : (k + 1) * LANES]
        for c in range(copies):
            emit[(c * tiles + k) * 8 : (c * tiles + k + 1) * 8, :] = block


def join_kernel(tiles, own_pos, own_nor, pos, nor, both):
    blocks = 2 * tiles
    for side, arrays in enumerate(((own_pos, own_nor), (pos, nor))):
        for v, array in enumerate(arrays):
            for k in range(tiles):
                both[pl.ds(3 * v * blocks + side * tiles + k, 3, stride=blocks), :] = array[
                    :, k * LANES : (k + 1) * LANES
                ]


def rank_kernel(tiles, n_row, n_col, owner, elem, basis, recv_list, emit_list, rank, slots, gram, recv_at, emit_at):
    my_pair, my_ring, my_core = (lax.axis_index(a) for a in ("pair", "ring", "core"))
    ring = n_row // 2
    step_of = -(-65536 // tiles)
    r = recv_list[...]
    q = (r * step_of) >> 16
    side = (q >= ring).astype(jnp.int32) ^ my_pair
    recv_at[...] = (((my_ring - q) & (ring - 1)) * 2 + side) * tiles + r - q * tiles
    e = emit_list[...]
    c = (e * step_of) >> 16
    emit_at[...] = ((c >> 1) + ((c ^ my_core) & 1) * (n_col // 2)) * tiles + e - c * tiles
    sub = lax.broadcasted_iota(jnp.int32, (LANES, LANES), 0)
    lane = lax.broadcasted_iota(jnp.int32, (LANES, LANES), 1)
    upper = jnp.concatenate([(sub < lane).astype(BF16), jnp.ones((LANES, LANES), BF16)], 1)
    carry = jnp.zeros((LANES, LANES), F32)
    found = jnp.zeros((LANES, 2 * LANES), F32)
    for g in range(tiles):
        named = owner[g : g + 1, :] == sub
        hot = jnp.where(named, 1.0, 0.0)
        counts = jnp.dot(hot.astype(BF16), upper, preferred_element_type=F32)
        place = jnp.sum(hot * (counts[:, :LANES] + carry), axis=0, keepdims=True)
        carry = carry + counts[:, LANES:]
        place = place.astype(jnp.int32)
        rank[g : g + 1, :] = place
        index = elem[g : g + 1, :]
        high = (index >> 7).astype(F32)
        low = (index & 127).astype(F32)
        at = place == sub
        table = jnp.concatenate([jnp.where(at, high, 0.0), jnp.where(at, low, 0.0)], 0)
        found = found + lax.dot_general(
            hot.astype(BF16), table.astype(BF16), NT, preferred_element_type=F32
        )
    slots[...] = found[:, :LANES] * 128.0 + found[:, LANES:]
    lanes = lax.broadcasted_iota(jnp.int32, (8, LANES), 1)
    subs = lax.broadcasted_iota(jnp.int32, (8, LANES), 0)
    total = jnp.zeros((8, LANES), F32)
    at = 0
    for i in range(8):
        sums = jnp.zeros((8, LANES), F32)
        for g in range(tiles):
            block = basis[:, g * LANES : (g + 1) * LANES]
            sums = sums + block * block[i : i + 1]
        value = jnp.sum(sums, axis=1, keepdims=True)
        total = total + jnp.where((subs >= i) & (lanes == at + subs - i), value, 0.0)
        at += 8 - i
    gram[...] = jnp.sum(total, axis=0, keepdims=True)


def receiver_kernel(*refs):
    wtab, consts_of = refs[-2:]
    row = lax.broadcasted_iota(jnp.int32, (8, LANES), 0)
    zero = jnp.zeros((8, LANES), F32)
    base = 0
    for recv in refs[:-2]:
        blocks = recv.shape[0] // 6
        x = [recv[f * blocks : (f + 1) * blocks, :] for f in range(6)]
        consts_of[0] = -(x[0] * x[3] + x[1] * x[4] + x[2] * x[5])
        consts_of[1] = x[0] * x[0] + x[1] * x[1] + x[2] * x[2]

        def body(k, _):
            block = jnp.concatenate(
                [recv[pl.ds(k, 6, stride=blocks), :]]
                + [consts_of[f, pl.ds(k, 1), :] for f in range(2)],
                0,
            )
            parts = split3(block)
            facing, away, spread = [], [], []
            for p, part in enumerate(parts):
                one = 1.0 if p == 0 else 0.0
                x_low = pltpu.roll(part, 3, 0)
                facing.append(jnp.where(row < 3, pltpu.roll(part, 5, 0), 0.0))
                away.append(jnp.where((row >= 3) & (row < 6), x_low, 0.0))
                spread.append(jnp.where(row < 3, -2.0 * part, jnp.where(row == 6, one, 0.0)))
            consts = []
            for f in (6, 7):
                h, m, l = (part[f : f + 1, :] for part in parts)
                consts.append(
                    jnp.where(row == 0, h, jnp.where(row == 1, m, jnp.where(row == 2, l, 0.0)))
                )
            ones = jnp.where((row >= 3) & (row < 6), 1.0, 0.0)
            for p, (w, c) in enumerate(
                ((facing, consts[0]), (away, ones), (spread, consts[1]))
            ):
                h, m, l = w
                wtab[base + k, :, p * LANES : (p + 1) * LANES] = jnp.concatenate(
                    [h, m, h, l, h, m, c, zero], 0
                ).astype(BF16)
            return 0

        lax.fori_loop(0, blocks, body, 0, unroll=8)
        base += blocks


def pair_kernel(tiles, n_row, n_col, unroll, count, recv_list, emit_list, near, far, wtab, out, etab, along, ratio, acc):
    row = lax.broadcasted_iota(jnp.int32, (8, LANES), 0)
    ones3 = jnp.where(row < 3, 1.0, 0.0)
    half = n_col // 2
    blocks = half * tiles
    ratios = []
    for s, source in enumerate((near, far)):
        feature = [source[pl.ds(f, blocks, stride=8), :] for f in range(8)]
        ratios.append(feature[7])
        total = -(feature[0] * feature[3] + feature[1] * feature[4] + feature[2] * feature[5])
        for p, part in enumerate(split3(total)):
            along[p, s * blocks : (s + 1) * blocks, :] = part
    ratios = jnp.concatenate(ratios, 0)
    for k in range(2 * blocks // LANES):
        ratio[k] = ratios[k * LANES : (k + 1) * LANES].T
    for s, source in enumerate((near, far)):

        def body(g, _):
            for k in range(tiles):
                at = g * tiles + k
                h, m, l = split3(source[pl.ds(pl.multiple_of(at * 8, 8), 8), :])
                ph, pm, pl_ = (along[p, pl.ds(s * blocks + at, 1), :] for p in range(3))
                tail = jnp.where(
                    row < 3,
                    1.0,
                    jnp.where(
                        row == 3, ph, jnp.where(row == 4, pm, jnp.where(row == 5, pl_, 0.0))
                    ),
                )
                etab[s * blocks + at] = jnp.concatenate(
                    [h, h, m, h, l, m, tail, jnp.zeros_like(tail)], 0
                ).astype(BF16)
            return 0

        lax.fori_loop(0, half, body, 0)
    acc[...] = jnp.zeros_like(acc)
    live = count[0]

    def fold(full):
        total = full[0:8]
        for k in range(1, LANES // 8):
            total = total + full[8 * k : 8 * k + 8]
        return total

    my_pair, my_ring = lax.axis_index("pair"), lax.axis_index("ring")
    ring = n_row // 2

    empty = jnp.zeros((64, 3 * LANES), BF16)

    def view(g, e):
        facing = jnp.maximum(g[:, :LANES], 0.0)
        away = jnp.maximum(g[:, LANES : 2 * LANES], 0.0)
        spread = g[:, 2 * LANES :]
        first = facing * away / (spread * spread)
        lane = jnp.full((LANES, LANES), e & (LANES - 1), jnp.int32)
        factor = jnp.take_along_axis(ratio[e >> 7], lane, axis=1, mode="promise_in_bounds")
        return fold(first), fold(first * factor)

    def two(at):
        r = recv_list[at], recv_list[at + 1]
        e = emit_list[at], emit_list[at + 1]
        weights = jnp.concatenate(
            [
                jnp.concatenate([wtab[r[0]], empty], 0),
                jnp.concatenate([empty, wtab[r[1]]], 0),
            ],
            1,
        )
        g = lax.dot_general(
            jnp.concatenate([etab[e[0]], etab[e[1]]], 0), weights, TN, preferred_element_type=F32
        )
        return [
            (r[k],) + view(g[:, 3 * k * LANES : 3 * (k + 1) * LANES], e[k]) for k in range(2)
        ]

    def step(i, _):
        found = []
        for k in range(0, unroll, 2):
            found += two(i * unroll + k)
        for k, (r, first, second) in enumerate(found):
            keep = jnp.where(i * unroll + k < live, 1.0, 0.0)
            at = pl.multiple_of(r * 16, 16)
            acc[pl.ds(at, 8), :] = acc[pl.ds(at, 8), :] + first * keep
            acc[pl.ds(at + 8, 8), :] = acc[pl.ds(at + 8, 8), :] + second * keep
        return 0

    lax.fori_loop(0, (live + unroll - 1) // unroll, step, 0)
    for q in range(n_row):
        target = (my_pair ^ (q & 1)) * ring + ((my_ring - (q >> 1)) & (ring - 1))
        for v in range(2):
            total = acc[pl.ds(q * tiles * 16 + v * 8, tiles, stride=16), :]
            for s in range(1, 8):
                total = total + acc[pl.ds(q * tiles * 16 + v * 8 + s, tiles, stride=16), :]
            at = pl.multiple_of((target * 2 + v) * tiles, 8)
            out[pl.ds(at, tiles), :] = total


def load_kernel(tiles, n_row, part, basis, mirrored, inner, area, owner, rank, slots, gram, message, damped):
    sub = lax.broadcasted_iota(jnp.int32, (LANES, LANES), 0)
    irradiance = part[0:tiles, :]
    scattered = part[tiles : 2 * tiles, :]
    for q in range(1, n_row):
        irradiance = irradiance + part[2 * q * tiles : (2 * q + 1) * tiles, :]
        scattered = scattered + part[(2 * q + 1) * tiles : (2 * q + 2) * tiles, :]
    fraction = mirrored[...]
    lost = fraction * scattered
    damped[...] = lost
    power = (1.0 - fraction) * irradiance + inner[...]
    load = 20.0 * area[...] * jnp.sqrt(jnp.sqrt(power))
    parts = split3(load)
    found = jnp.zeros((LANES, LANES), F32)
    for begin in range(0, tiles, 4):
        hots, tables = [], []
        for g in range(begin, begin + 4):
            hots += [jnp.where(owner[g : g + 1, :] == sub, 1.0, 0.0).astype(BF16)] * 3
            at = rank[g : g + 1, :] == sub
            tables += [jnp.where(at, v[g : g + 1, :], 0.0).astype(BF16) for v in parts]
        found = found + lax.dot_general(
            jnp.concatenate(hots, 1), jnp.concatenate(tables, 1), NT, preferred_element_type=F32
        )
    lanes = lax.broadcasted_iota(jnp.int32, (8, LANES), 1)
    subs = lax.broadcasted_iota(jnp.int32, (8, LANES), 0)
    sums = jnp.zeros((8, LANES), F32)
    for g in range(tiles):
        sums = sums + basis[:, g * LANES : (g + 1) * LANES] * lost[g : g + 1, :]
    inner_products = jnp.sum(sums, axis=1, keepdims=True)
    square = jnp.sum(lost * lost, axis=(0, 1), keepdims=True)
    stats = jnp.sum(
        jnp.where(lanes == 96 + subs, inner_products, 0.0), axis=0, keepdims=True
    )
    g = jnp.broadcast_to(gram[...], (8, LANES))
    lane = lanes[0:1]
    stats = jnp.where(lane == 104, square, stats)
    stats = jnp.where(lane >= 105, pltpu.roll(g, 105, 1)[0:1], stats)
    more = pltpu.roll(g, 73, 1)[0:1]
    keep = lax.broadcasted_iota(jnp.int32, (LANES, LANES), 1) < 96
    message[pl.ds(0, LANES, stride=2), :] = jnp.where(keep, found, stats)
    message[pl.ds(1, LANES, stride=2), :] = jnp.where(keep, slots[...], more)


def finish_kernel(tiles, cells, arrived, basis, damped, vector, hessen, loads, value_rows, index_rows):
    values = arrived[pl.ds(0, LANES, stride=2), :]
    second = arrived[pl.ds(1, LANES, stride=2), :]
    top = jnp.sum(values, axis=0, keepdims=True)
    low = jnp.sum(second, axis=0, keepdims=True)
    inner = [top[:, 96 + k : 97 + k] for k in range(8)]
    lost_square = top[:, 104:105]
    gram = {}
    at = 0
    for i in range(8):
        for j in range(i, 8):
            lane = 105 + at
            gram[i, j] = top[:, lane : lane + 1] if lane < 128 else low[:, lane - 32 : lane - 31]
            gram[j, i] = gram[i, j]
            at += 1
    scale = 1.0 / cells
    coeffs = [(gram[7, k] - inner[k]) * scale for k in range(8)]
    left = [(1.0 if k == 7 else 0.0) - coeffs[k] for k in range(8)]
    square = lost_square
    for i in range(8):
        line = gram[i, i] * left[i] - 2.0 * inner[i]
        for j in range(i + 1, 8):
            line = line + 2.0 * gram[i, j] * left[j]
        square = square + line * left[i]
    length = jnp.sqrt(jnp.maximum(square, 0.0) * scale + 1e-6)
    inverse = 1.0 / length
    subs = lax.broadcasted_iota(jnp.int32, (8, LANES), 0)
    weights = jnp.zeros((8, LANES), F32)
    for k in range(8):
        weights = jnp.where(subs == k, left[k], weights)
    for g in range(tiles):
        mixed = jnp.sum(basis[:, g * LANES : (g + 1) * LANES] * weights, axis=0, keepdims=True)
        vector[g : g + 1, :] = (mixed - damped[g : g + 1, :]) * inverse
    lanes = lax.broadcasted_iota(jnp.int32, (1, LANES), 1)
    column = jnp.where(lanes == 8, length, 0.0)
    for k in range(8):
        column = jnp.where(lanes == k, coeffs[k], column)
    hessen[...] = column[:, 0:9]
    keep = lax.broadcasted_iota(jnp.int32, (LANES, LANES), 1) < 96
    for k, v in enumerate(split3(jnp.where(keep, values, 0.0))):
        value_rows[k] = v
    index_rows[...] = second.astype(jnp.int32)
    sub = lax.broadcasted_iota(jnp.int32, (LANES, LANES), 0)
    sub16 = lax.broadcasted_iota(jnp.int32, (16, LANES), 0)
    total = jnp.zeros((48, LANES), F32)
    for s in range(0, LANES, 8):
        left_side, right_side = [], []
        for u in range(s, s + 8):
            index = index_rows[u : u + 1, :]
            mask = (index >> 7) == sub16
            left_side.append(
                jnp.concatenate(
                    [jnp.where(mask, value_rows[k, u : u + 1, :], 0.0) for k in range(3)], 0
                ).astype(BF16)
            )
            right_side.append(jnp.where((index & 127) == sub, 1.0, 0.0).astype(BF16))
        total = total + lax.dot_general(
            jnp.concatenate(left_side, 1),
            jnp.concatenate(right_side, 1),
            NT,
            preferred_element_type=F32,
        )
    loads[...] = total[0:16] + total[16:32] + total[32:48]


def shards(
    positions,
    normals,
    patch_extents,
    mirrored_fraction,
    inner_emission_power,
    radiosity,
    basis,
    recv_blocks,
    emit_blocks,
    vis_count,
    owner,
    local_elem,
):
    patches = positions.shape[1]
    tiles = patches // LANES
    pairs_of, ring, half, cores = (lax.axis_size(a) for a in AXES)
    n_row, n_col = pairs_of * ring, half * cores
    devices = n_row * n_col
    shape = jax.ShapeDtypeStruct

    def rows(array):
        return array.reshape(-1, LANES)

    hbm = pl.BlockSpec(memory_space=pl.ANY)
    swap = [(0, 1), (1, 0)]
    swapped = [lax.ppermute(array, "pair", swap) for array in (positions, normals)]
    emit = call(
        functools.partial(emit_kernel, tiles, half),
        shape((half * 8 * tiles, LANES), F32),
        scratch=[
            pltpu.VMEM((3, patches), F32),
            pltpu.VMEM((3, patches), F32),
            pltpu.VMEM((1, patches), F32),
            pltpu.VMEM((1, patches), F32),
            pltpu.VMEM((8, patches), F32),
            pltpu.SemaphoreType.DMA((5,)),
        ],
        in_specs=[hbm] * 5,
        name="emit",
        micros=4,
        limit=60 * 2**20,
    )(positions, normals, patch_extents[None], radiosity[None], basis)
    emit, swapped = lax.optimization_barrier((emit, swapped))
    both = call(
        functools.partial(join_kernel, tiles),
        shape((12 * tiles, LANES), F32),
        in_specs=[VMEM] * 4,
        name="join",
        micros=3,
    )(positions, normals, *swapped)
    owner_rows, both_again = lax.optimization_barrier((rows(owner), both))
    lists = rows(recv_blocks), rows(emit_blocks)
    rank, slots, gram, recv_at, emit_at = call(
        functools.partial(rank_kernel, tiles, n_row, n_col),
        (
            shape((tiles, LANES), jnp.int32),
            shape((LANES, LANES), F32),
            shape((1, LANES), F32),
            shape(lists[0].shape, jnp.int32),
            shape(lists[1].shape, jnp.int32),
        ),
        in_specs=[VMEM] * 5,
        name="rank",
        micros=3,
        limit=60 * 2**20,
    )(owner_rows, rows(local_elem), basis, *lists)
    received = [both_again] + [
        lax.ppermute(both, "ring", [(i, (i + k) % ring) for i in range(ring)])
        for k in range(1, ring)
    ]
    near = rows(lax.all_to_all(emit.reshape(half, -1), "half", 0, 0, tiled=True))
    near, received, recv_at, emit_at = lax.optimization_barrier(
        (near, received, recv_at, emit_at)
    )
    far = lax.ppermute(near, "core", [(0, 1), (1, 0)])
    wtab = call(
        receiver_kernel,
        shape((n_row * tiles, 64, 3 * LANES), BF16),
        scratch=[pltpu.VMEM((2, 2 * tiles, LANES), F32)],
        in_specs=[VMEM] * len(received),
        name="receivers",
        micros=4,
    )(*received)
    unroll = 64
    part = call(
        functools.partial(pair_kernel, tiles, n_row, n_col, unroll),
        shape((n_row * 2 * tiles, LANES), F32),
        scratch=[
            pltpu.VMEM((n_col * tiles, 64, LANES), BF16),
            pltpu.VMEM((3, n_col * tiles, LANES), F32),
            pltpu.VMEM((n_col * tiles // LANES, LANES, LANES), F32),
            pltpu.VMEM((n_row * tiles * 16, LANES), F32),
        ],
        in_specs=[SMEM] * 3 + [VMEM] * 3,
        name="pairs",
        micros=20,
    )(
        vis_count.reshape(-1),
        recv_at.reshape(-1),
        emit_at.reshape(-1),
        near,
        far,
        wtab,
    )
    part = lax.all_to_all(part.reshape(n_row, -1), ROW, 0, 0, tiled=True)
    message, damped = call(
        functools.partial(load_kernel, tiles, n_row),
        (shape((2 * devices, LANES), F32), shape((tiles, LANES), F32)),
        in_specs=[VMEM] * 9,
        name="loads",
    )(
        rows(part),
        basis,
        rows(mirrored_fraction),
        rows(inner_emission_power),
        rows(patch_extents),
        owner_rows,
        rank,
        slots,
        gram,
    )
    arrived = lax.all_to_all(message.reshape(devices, -1), AXES, 0, 0, tiled=True)
    vector, hessen, loads = call(
        functools.partial(finish_kernel, tiles, float(patches * devices)),
        (
            shape((tiles, LANES), F32),
            shape((1, 9), F32),
            shape((E_DEV // LANES, LANES), F32),
        ),
        scratch=[pltpu.VMEM((3, LANES, LANES), F32), pltpu.VMEM((LANES, LANES), jnp.int32)],
        in_specs=[VMEM] * 3,
        name="finish",
    )(rows(arrived), basis, damped)
    return vector.reshape(-1), hessen.reshape(-1), loads.reshape(-1)


def solution(mesh):
    n_row, n_col = mesh.shape["row"], mesh.shape["col"]
    fine = Mesh(mesh.devices.reshape(2, n_row // 2, n_col // 2, 2), AXES)
    every = P(AXES)
    second = P(None, AXES)
    grid = P(ROW, ("half", "core"))
    in_specs = (
        second,
        second,
        every,
        every,
        every,
        every,
        second,
        P(ROW, ("half", "core"), None),
        P(ROW, ("half", "core"), None),
        grid,
        P(AXES, None),
        every,
    )
    return jax.shard_map(
        shards, mesh=fine, in_specs=in_specs, out_specs=(every, P(), every), check_vma=False
    )
```

```python
import functools
import math

import jax
import jax.numpy as jnp
from jax import lax
from jax.experimental import pallas as pl
from jax.experimental.pallas import tpu as pltpu
from jax.sharding import Mesh, PartitionSpec as P

F32 = jnp.float32
BF16 = jnp.bfloat16
LANES = 128
AXES = ("pair", "ring", "half", "core")
ROW = ("pair", "ring")
E_DEV = 2048
NT = (((1,), (1,)), ((), ()))
TN = (((0,), (0,)), ((), ()))
VMEM = pl.BlockSpec(memory_space=pltpu.VMEM)
SMEM = pl.BlockSpec(memory_space=pltpu.SMEM)
LIMIT = 32 * 2**20


def split3(value):
    high = value.astype(BF16).astype(F32)
    rest = value - high
    middle = rest.astype(BF16).astype(F32)
    return high, middle, rest - middle


def call(body, out_shape, scratch=(), in_specs=None, name=None, micros=1, limit=LIMIT):
    return pl.pallas_call(
        body,
        out_shape=out_shape,
        in_specs=in_specs,
        out_specs=jax.tree.map(lambda _: VMEM, out_shape),
        scratch_shapes=list(scratch),
        compiler_params=pltpu.CompilerParams(vmem_limit_bytes=limit),
        cost_estimate=pl.CostEstimate(
            flops=int(micros * 1.1e9), bytes_accessed=2**16, transcendentals=0
        ),
        name=name,
    )


def fetch(sources, targets, sems):
    moves = [
        pltpu.make_async_copy(source, target, sems.at[k])
        for k, (source, target) in enumerate(zip(sources, targets))
    ]
    for move in moves:
        move.start()
    for move in moves:
        move.wait()


def emit_kernel(tiles, copies, pos, nor, area, rad, basis, emit, pos_v, nor_v, area_v, rad_v, basis_v, sems):
    fetch((pos, nor, area, rad, basis), (pos_v, nor_v, area_v, rad_v, basis_v), sems)
    x = pos_v[...]
    n = nor_v[...]
    a = area_v[...]
    b = rad_v[...]
    m = (a * b * (1.0 / math.pi)) * n
    square = x * x
    square = square[0:1] + square[1:2] + square[2:3]
    emit_rows = jnp.concatenate([x, m, square + a, basis_v[7:8, :] / b], 0)
    for k in range(tiles):
        block = emit_rows[:, k * LANES : (k + 1) * LANES]
        for c in range(copies):
            emit[(c * tiles + k) * 8 : (c * tiles + k + 1) * 8, :] = block


def join_kernel(tiles, own_pos, own_nor, pos, nor, both):
    blocks = 2 * tiles
    for side, arrays in enumerate(((own_pos, own_nor), (pos, nor))):
        for v, array in enumerate(arrays):
            for f in range(3):
                base = (3 * v + f) * blocks + side * tiles
                for k in range(tiles):
                    both[base + k : base + k + 1, :] = array[
                        f : f + 1, k * LANES : (k + 1) * LANES
                    ]


def rank_kernel(tiles, n_row, n_col, place, owner, elem, basis, recv_list, emit_list, rank, slots, gram, recv_at, emit_at):
    my_pair, my_ring, my_core = place[0], place[1], place[2]
    ring = n_row // 2
    step_of = -(-65536 // tiles)
    r = recv_list[...]
    q = (r * step_of) >> 16
    side = (q >= ring).astype(jnp.int32) ^ my_pair
    recv_at[...] = (((my_ring - q) & (ring - 1)) * 2 + side) * tiles + r - q * tiles
    e = emit_list[...]
    c = (e * step_of) >> 16
    emit_at[...] = ((c >> 1) + ((c ^ my_core) & 1) * (n_col // 2)) * tiles + e - c * tiles
    sub = lax.broadcasted_iota(jnp.int32, (LANES, LANES), 0)
    lane = lax.broadcasted_iota(jnp.int32, (LANES, LANES), 1)
    upper = jnp.concatenate([(sub < lane).astype(BF16), jnp.ones((LANES, LANES), BF16)], 1)
    carry = jnp.zeros((LANES, LANES), F32)
    found = jnp.zeros((LANES, 2 * LANES), F32)
    for g in range(tiles):
        named = owner[g : g + 1, :] == sub
        hot = jnp.where(named, 1.0, 0.0)
        counts = jnp.dot(hot.astype(BF16), upper, preferred_element_type=F32)
        place = jnp.sum(hot * (counts[:, :LANES] + carry), axis=0, keepdims=True)
        carry = carry + counts[:, LANES:]
        place = place.astype(jnp.int32)
        rank[g : g + 1, :] = place
        index = elem[g : g + 1, :]
        high = (index >> 7).astype(F32)
        low = (index & 127).astype(F32)
        at = place == sub
        table = jnp.concatenate([jnp.where(at, high, 0.0), jnp.where(at, low, 0.0)], 0)
        found = found + lax.dot_general(
            hot.astype(BF16), table.astype(BF16), NT, preferred_element_type=F32
        )
    slots[...] = found[:, :LANES] * 128.0 + found[:, LANES:]
    lanes = lax.broadcasted_iota(jnp.int32, (8, LANES), 1)
    subs = lax.broadcasted_iota(jnp.int32, (8, LANES), 0)
    total = jnp.zeros((8, LANES), F32)
    at = 0
    for i in range(8):
        sums = jnp.zeros((8, LANES), F32)
        for g in range(tiles):
            block = basis[:, g * LANES : (g + 1) * LANES]
            sums = sums + block * block[i : i + 1]
        value = jnp.sum(sums, axis=1, keepdims=True)
        total = total + jnp.where((subs >= i) & (lanes == at + subs - i), value, 0.0)
        at += 8 - i
    gram[...] = jnp.sum(total, axis=0, keepdims=True)


def receiver_kernel(*refs):
    wtab, features = refs[-2:]
    row = lax.broadcasted_iota(jnp.int32, (8, LANES), 0)
    zero = jnp.zeros((8, LANES), F32)
    base = 0
    for recv in refs[:-2]:
        blocks = recv.shape[0] // 6
        x = [recv[f * blocks : (f + 1) * blocks, :] for f in range(6)]
        x.append(-(x[0] * x[3] + x[1] * x[4] + x[2] * x[5]))
        x.append(x[0] * x[0] + x[1] * x[1] + x[2] * x[2])
        for f in range(8):
            features[pl.ds(f, blocks, stride=8), :] = x[f]

        def body(k, _):
            block = features[pl.ds(pl.multiple_of(k * 8, 8), 8), :]
            parts = split3(block)
            facing, away, spread = [], [], []
            for p, part in enumerate(parts):
                one = 1.0 if p == 0 else 0.0
                x_low = pltpu.roll(part, 3, 0)
                facing.append(jnp.where(row < 3, pltpu.roll(part, 5, 0), 0.0))
                away.append(jnp.where((row >= 3) & (row < 6), x_low, 0.0))
                spread.append(jnp.where(row < 3, -2.0 * part, jnp.where(row == 6, one, 0.0)))
            consts = []
            for f in (6, 7):
                h, m, l = (part[f : f + 1, :] for part in parts)
                consts.append(
                    jnp.where(row == 0, h, jnp.where(row == 1, m, jnp.where(row == 2, l, 0.0)))
                )
            ones = jnp.where((row >= 3) & (row < 6), 1.0, 0.0)
            for p, (w, c) in enumerate(
                ((facing, consts[0]), (away, ones), (spread, consts[1]))
            ):
                h, m, l = w
                wtab[base + k, :, p * LANES : (p + 1) * LANES] = jnp.concatenate(
                    [h, m, h, l, h, m, c, zero], 0
                ).astype(BF16)
            return 0

        lax.fori_loop(0, blocks, body, 0, unroll=8)
        base += blocks


def pair_kernel(tiles, n_row, n_col, unroll, count, recv_list, emit_list, place, near, far, wtab, out, etab, along, ratio, acc):
    row = lax.broadcasted_iota(jnp.int32, (8, LANES), 0)
    ones3 = jnp.where(row < 3, 1.0, 0.0)
    half = n_col // 2
    blocks = half * tiles
    ratios = []
    for s, source in enumerate((near, far)):
        feature = [source[pl.ds(f, blocks, stride=8), :] for f in range(8)]
        ratios.append(feature[7])
        total = -(feature[0] * feature[3] + feature[1] * feature[4] + feature[2] * feature[5])
        for p, part in enumerate(split3(total)):
            along[p, s * blocks : (s + 1) * blocks, :] = part
    ratios = jnp.concatenate(ratios, 0)
    for k in range(2 * blocks // LANES):
        ratio[k] = ratios[k * LANES : (k + 1) * LANES].T
    for s, source in enumerate((near, far)):

        def body(g, _):
            for k in range(tiles):
                at = g * tiles + k
                h, m, l = split3(source[pl.ds(pl.multiple_of(at * 8, 8), 8), :])
                ph, pm, pl_ = (along[p, pl.ds(s * blocks + at, 1), :] for p in range(3))
                tail = jnp.where(
                    row < 3,
                    1.0,
                    jnp.where(
                        row == 3, ph, jnp.where(row == 4, pm, jnp.where(row == 5, pl_, 0.0))
                    ),
                )
                etab[s * blocks + at] = jnp.concatenate(
                    [h, h, m, h, l, m, tail, jnp.zeros_like(tail)], 0
                ).astype(BF16)
            return 0

        lax.fori_loop(0, half, body, 0)
    acc[...] = jnp.zeros_like(acc)
    live = count[0]

    def fold(full):
        total = full[0:8]
        for k in range(1, LANES // 8):
            total = total + full[8 * k : 8 * k + 8]
        return total

    my_pair, my_ring = place[0], place[1]
    ring = n_row // 2

    empty = jnp.zeros((64, 3 * LANES), BF16)

    def view(g, e):
        facing = jnp.maximum(g[:, :LANES], 0.0)
        away = jnp.maximum(g[:, LANES : 2 * LANES], 0.0)
        spread = g[:, 2 * LANES :]
        first = facing * away / (spread * spread)
        lane = jnp.full((LANES, LANES), e & (LANES - 1), jnp.int32)
        factor = jnp.take_along_axis(ratio[e >> 7], lane, axis=1, mode="promise_in_bounds")
        return fold(first), fold(first * factor)

    def two(at):
        r = recv_list[at], recv_list[at + 1]
        e = emit_list[at], emit_list[at + 1]
        weights = jnp.concatenate(
            [
                jnp.concatenate([wtab[r[0]], empty], 0),
                jnp.concatenate([empty, wtab[r[1]]], 0),
            ],
            1,
        )
        g = lax.dot_general(
            jnp.concatenate([etab[e[0]], etab[e[1]]], 0), weights, TN, preferred_element_type=F32
        )
        return [
            (r[k],) + view(g[:, 3 * k * LANES : 3 * (k + 1) * LANES], e[k]) for k in range(2)
        ]

    def step(i, _):
        found = []
        for k in range(0, unroll, 2):
            found += two(i * unroll + k)
        for k, (r, first, second) in enumerate(found):
            keep = jnp.where(i * unroll + k < live, 1.0, 0.0)
            at = pl.multiple_of(r * 16, 16)
            acc[pl.ds(at, 8), :] = acc[pl.ds(at, 8), :] + first * keep
            acc[pl.ds(at + 8, 8), :] = acc[pl.ds(at + 8, 8), :] + second * keep
        return 0

    lax.fori_loop(0, (live + unroll - 1) // unroll, step, 0)
    for q in range(n_row):
        target = (my_pair ^ (q & 1)) * ring + ((my_ring - (q >> 1)) & (ring - 1))
        for v in range(2):
            total = acc[pl.ds(q * tiles * 16 + v * 8, tiles, stride=16), :]
            for s in range(1, 8):
                total = total + acc[pl.ds(q * tiles * 16 + v * 8 + s, tiles, stride=16), :]
            at = pl.multiple_of((target * 2 + v) * tiles, 8)
            out[pl.ds(at, tiles), :] = total


def load_kernel(tiles, n_row, part, basis, mirrored, inner, area, owner, rank, slots, gram, message, damped):
    sub = lax.broadcasted_iota(jnp.int32, (LANES, LANES), 0)
    irradiance = part[0:tiles, :]
    scattered = part[tiles : 2 * tiles, :]
    for q in range(1, n_row):
        irradiance = irradiance + part[2 * q * tiles : (2 * q + 1) * tiles, :]
        scattered = scattered + part[(2 * q + 1) * tiles : (2 * q + 2) * tiles, :]
    fraction = mirrored[...]
    lost = fraction * scattered
    damped[...] = lost
    power = (1.0 - fraction) * irradiance + inner[...]
    load = 20.0 * area[...] * jnp.sqrt(jnp.sqrt(power))
    parts = split3(load)
    found = jnp.zeros((LANES, LANES), F32)
    for begin in range(0, tiles, 4):
        hots, tables = [], []
        for g in range(begin, begin + 4):
            hots += [jnp.where(owner[g : g + 1, :] == sub, 1.0, 0.0).astype(BF16)] * 3
            at = rank[g : g + 1, :] == sub
            tables += [jnp.where(at, v[g : g + 1, :], 0.0).astype(BF16) for v in parts]
        found = found + lax.dot_general(
            jnp.concatenate(hots, 1), jnp.concatenate(tables, 1), NT, preferred_element_type=F32
        )
    lanes = lax.broadcasted_iota(jnp.int32, (8, LANES), 1)
    subs = lax.broadcasted_iota(jnp.int32, (8, LANES), 0)
    sums = jnp.zeros((8, LANES), F32)
    for g in range(tiles):
        sums = sums + basis[:, g * LANES : (g + 1) * LANES] * lost[g : g + 1, :]
    inner_products = jnp.sum(sums, axis=1, keepdims=True)
    square = jnp.sum(lost * lost, axis=(0, 1), keepdims=True)
    stats = jnp.sum(
        jnp.where(lanes == 96 + subs, inner_products, 0.0), axis=0, keepdims=True
    )
    g = jnp.broadcast_to(gram[...], (8, LANES))
    lane = lanes[0:1]
    stats = jnp.where(lane == 104, square, stats)
    stats = jnp.where(lane >= 105, pltpu.roll(g, 105, 1)[0:1], stats)
    more = pltpu.roll(g, 73, 1)[0:1]
    keep = lax.broadcasted_iota(jnp.int32, (LANES, LANES), 1) < 96
    message[pl.ds(0, LANES, stride=2), :] = jnp.where(keep, found, stats)
    message[pl.ds(1, LANES, stride=2), :] = jnp.where(keep, slots[...], more)


def finish_kernel(tiles, cells, arrived, basis, damped, vector, hessen, loads, value_rows, index_rows):
    values = arrived[pl.ds(0, LANES, stride=2), :]
    second = arrived[pl.ds(1, LANES, stride=2), :]
    top = jnp.sum(values, axis=0, keepdims=True)
    low = jnp.sum(second, axis=0, keepdims=True)
    inner = [top[:, 96 + k : 97 + k] for k in range(8)]
    lost_square = top[:, 104:105]
    gram = {}
    at = 0
    for i in range(8):
        for j in range(i, 8):
            lane = 105 + at
            gram[i, j] = top[:, lane : lane + 1] if lane < 128 else low[:, lane - 32 : lane - 31]
            gram[j, i] = gram[i, j]
            at += 1
    scale = 1.0 / cells
    coeffs = [(gram[7, k] - inner[k]) * scale for k in range(8)]
    left = [(1.0 if k == 7 else 0.0) - coeffs[k] for k in range(8)]
    square = lost_square
    for i in range(8):
        line = gram[i, i] * left[i] - 2.0 * inner[i]
        for j in range(i + 1, 8):
            line = line + 2.0 * gram[i, j] * left[j]
        square = square + line * left[i]
    length = jnp.sqrt(jnp.maximum(square, 0.0) * scale + 1e-6)
    inverse = 1.0 / length
    subs = lax.broadcasted_iota(jnp.int32, (8, LANES), 0)
    weights = jnp.zeros((8, LANES), F32)
    for k in range(8):
        weights = jnp.where(subs == k, left[k], weights)
    for g in range(tiles):
        mixed = jnp.sum(basis[:, g * LANES : (g + 1) * LANES] * weights, axis=0, keepdims=True)
        vector[g : g + 1, :] = (mixed - damped[g : g + 1, :]) * inverse
    lanes = lax.broadcasted_iota(jnp.int32, (1, LANES), 1)
    column = jnp.where(lanes == 8, length, 0.0)
    for k in range(8):
        column = jnp.where(lanes == k, coeffs[k], column)
    hessen[...] = column[:, 0:9]
    keep = lax.broadcasted_iota(jnp.int32, (LANES, LANES), 1) < 96
    for k, v in enumerate(split3(jnp.where(keep, values, 0.0))):
        value_rows[k] = v
    index_rows[...] = second.astype(jnp.int32)
    sub = lax.broadcasted_iota(jnp.int32, (LANES, LANES), 0)
    sub16 = lax.broadcasted_iota(jnp.int32, (16, LANES), 0)
    total = jnp.zeros((48, LANES), F32)
    for s in range(0, LANES, 8):
        left_side, right_side = [], []
        for u in range(s, s + 8):
            index = index_rows[u : u + 1, :]
            mask = (index >> 7) == sub16
            left_side.append(
                jnp.concatenate(
                    [jnp.where(mask, value_rows[k, u : u + 1, :], 0.0) for k in range(3)], 0
                ).astype(BF16)
            )
            right_side.append(jnp.where((index & 127) == sub, 1.0, 0.0).astype(BF16))
        total = total + lax.dot_general(
            jnp.concatenate(left_side, 1),
            jnp.concatenate(right_side, 1),
            NT,
            preferred_element_type=F32,
        )
    loads[...] = total[0:16] + total[16:32] + total[32:48]


def shards(
    positions,
    normals,
    patch_extents,
    mirrored_fraction,
    inner_emission_power,
    radiosity,
    basis,
    recv_blocks,
    emit_blocks,
    vis_count,
    owner,
    local_elem,
):
    patches = positions.shape[1]
    tiles = patches // LANES
    pairs_of, ring, half, cores = (lax.axis_size(a) for a in AXES)
    n_row, n_col = pairs_of * ring, half * cores
    devices = n_row * n_col
    place = jnp.stack([lax.axis_index(a) for a in ("pair", "ring", "core")])
    shape = jax.ShapeDtypeStruct

    def rows(array):
        return array.reshape(-1, LANES)

    hbm = pl.BlockSpec(memory_space=pl.ANY)
    swap = [(0, 1), (1, 0)]
    swapped = [lax.ppermute(array, "pair", swap) for array in (positions, normals)]
    emit = call(
        functools.partial(emit_kernel, tiles, half),
        shape((half * 8 * tiles, LANES), F32),
        scratch=[
            pltpu.VMEM((3, patches), F32),
            pltpu.VMEM((3, patches), F32),
            pltpu.VMEM((1, patches), F32),
            pltpu.VMEM((1, patches), F32),
            pltpu.VMEM((8, patches), F32),
            pltpu.SemaphoreType.DMA((5,)),
        ],
        in_specs=[hbm] * 5,
        name="emit",
        micros=4,
        limit=60 * 2**20,
    )(positions, normals, patch_extents[None], radiosity[None], basis)
    both = call(
        functools.partial(join_kernel, tiles),
        shape((12 * tiles, LANES), F32),
        in_specs=[VMEM] * 4,
        name="join",
        micros=3,
    )(positions, normals, *swapped)
    owner_rows, both_again = lax.optimization_barrier((rows(owner), both))
    lists = rows(recv_blocks), rows(emit_blocks)
    rank, slots, gram, recv_at, emit_at = call(
        functools.partial(rank_kernel, tiles, n_row, n_col),
        (
            shape((tiles, LANES), jnp.int32),
            shape((LANES, LANES), F32),
            shape((1, LANES), F32),
            shape(lists[0].shape, jnp.int32),
            shape(lists[1].shape, jnp.int32),
        ),
        in_specs=[SMEM] + [VMEM] * 5,
        name="rank",
        micros=3,
        limit=60 * 2**20,
    )(place, owner_rows, rows(local_elem), basis, *lists)
    received = [both_again] + [
        lax.ppermute(both, "ring", [(i, (i + k) % ring) for i in range(ring)])
        for k in range(1, ring)
    ]
    near = rows(lax.all_to_all(emit.reshape(half, -1), "half", 0, 0, tiled=True))
    near, received, recv_at, emit_at = lax.optimization_barrier(
        (near, received, recv_at, emit_at)
    )
    far = lax.ppermute(near, "core", [(0, 1), (1, 0)])
    wtab = call(
        receiver_kernel,
        shape((n_row * tiles, 64, 3 * LANES), BF16),
        scratch=[pltpu.VMEM((16 * tiles, LANES), F32)],
        in_specs=[VMEM] * len(received),
        name="receivers",
        micros=4,
    )(*received)
    unroll = 64
    part = call(
        functools.partial(pair_kernel, tiles, n_row, n_col, unroll),
        shape((n_row * 2 * tiles, LANES), F32),
        scratch=[
            pltpu.VMEM((n_col * tiles, 64, LANES), BF16),
            pltpu.VMEM((3, n_col * tiles, LANES), F32),
            pltpu.VMEM((n_col * tiles // LANES, LANES, LANES), F32),
            pltpu.VMEM((n_row * tiles * 16, LANES), F32),
        ],
        in_specs=[SMEM] * 4 + [VMEM] * 3,
        name="pairs",
        micros=20,
    )(
        vis_count.reshape(-1),
        recv_at.reshape(-1),
        emit_at.reshape(-1),
        place,
        near,
        far,
        wtab,
    )
    part = lax.all_to_all(part.reshape(n_row, -1), ROW, 0, 0, tiled=True)
    message, damped = call(
        functools.partial(load_kernel, tiles, n_row),
        (shape((2 * devices, LANES), F32), shape((tiles, LANES), F32)),
        in_specs=[VMEM] * 9,
        name="loads",
    )(
        rows(part),
        basis,
        rows(mirrored_fraction),
        rows(inner_emission_power),
        rows(patch_extents),
        owner_rows,
        rank,
        slots,
        gram,
    )
    arrived = lax.all_to_all(message.reshape(devices, -1), AXES, 0, 0, tiled=True)
    vector, hessen, loads = call(
        functools.partial(finish_kernel, tiles, float(patches * devices)),
        (
            shape((tiles, LANES), F32),
            shape((1, 9), F32),
            shape((E_DEV // LANES, LANES), F32),
        ),
        scratch=[pltpu.VMEM((3, LANES, LANES), F32), pltpu.VMEM((LANES, LANES), jnp.int32)],
        in_specs=[VMEM] * 3,
        name="finish",
    )(rows(arrived), basis, damped)
    return vector.reshape(-1), hessen.reshape(-1), loads.reshape(-1)


def solution(mesh):
    n_row, n_col = mesh.shape["row"], mesh.shape["col"]
    fine = Mesh(mesh.devices.reshape(2, n_row // 2, n_col // 2, 2), AXES)
    every = P(AXES)
    second = P(None, AXES)
    grid = P(ROW, ("half", "core"))
    in_specs = (
        second,
        second,
        every,
        every,
        every,
        every,
        second,
        P(ROW, ("half", "core"), None),
        P(ROW, ("half", "core"), None),
        grid,
        P(AXES, None),
        every,
    )
    return jax.shard_map(
        shards, mesh=fine, in_specs=in_specs, out_specs=(every, P(), every), check_vma=False
    )
```

```python
import functools
import math

import jax
import jax.numpy as jnp
from jax import lax
from jax.experimental import pallas as pl
from jax.experimental.pallas import tpu as pltpu
from jax.sharding import Mesh, PartitionSpec as P

F32 = jnp.float32
BF16 = jnp.bfloat16
LANES = 128
AXES = ("pair", "ring", "half", "core")
ROW = ("pair", "ring")
E_DEV = 2048
NT = (((1,), (1,)), ((), ()))
TN = (((0,), (0,)), ((), ()))
VMEM = pl.BlockSpec(memory_space=pltpu.VMEM)
SMEM = pl.BlockSpec(memory_space=pltpu.SMEM)
LIMIT = 32 * 2**20


def split3(value):
    high = value.astype(BF16).astype(F32)
    rest = value - high
    middle = rest.astype(BF16).astype(F32)
    return high, middle, rest - middle


def call(body, out_shape, scratch=(), in_specs=None, name=None, micros=1, limit=LIMIT):
    return pl.pallas_call(
        body,
        out_shape=out_shape,
        in_specs=in_specs,
        out_specs=jax.tree.map(lambda _: VMEM, out_shape),
        scratch_shapes=list(scratch),
        compiler_params=pltpu.CompilerParams(vmem_limit_bytes=limit),
        cost_estimate=pl.CostEstimate(
            flops=int(micros * 1.1e9), bytes_accessed=2**16, transcendentals=0
        ),
        name=name,
    )


def fetch(sources, targets, sems):
    moves = [
        pltpu.make_async_copy(source, target, sems.at[k])
        for k, (source, target) in enumerate(zip(sources, targets))
    ]
    for move in moves:
        move.start()
    for move in moves:
        move.wait()


def emit_kernel(tiles, copies, pos, nor, area, rad, basis, emit, pos_v, nor_v, area_v, rad_v, basis_v, sems):
    fetch((pos, nor, area, rad, basis), (pos_v, nor_v, area_v, rad_v, basis_v), sems)
    x = pos_v[...]
    n = nor_v[...]
    a = area_v[...]
    b = rad_v[...]
    m = (a * b * (1.0 / math.pi)) * n
    square = x * x
    square = square[0:1] + square[1:2] + square[2:3]
    emit_rows = jnp.concatenate([x, m, square + a, basis_v[7:8, :] / b], 0)
    for k in range(tiles):
        block = emit_rows[:, k * LANES : (k + 1) * LANES]
        for c in range(copies):
            emit[(c * tiles + k) * 8 : (c * tiles + k + 1) * 8, :] = block


def join_kernel(tiles, own_pos, own_nor, pos, nor, both):
    blocks = 2 * tiles
    for side, arrays in enumerate(((own_pos, own_nor), (pos, nor))):
        for v, array in enumerate(arrays):
            for f in range(3):
                base = (3 * v + f) * blocks + side * tiles
                for k in range(tiles):
                    both[base + k : base + k + 1, :] = array[
                        f : f + 1, k * LANES : (k + 1) * LANES
                    ]


def rank_kernel(tiles, n_row, n_col, place, owner, elem, basis, recv_list, emit_list, rank, slots, gram, recv_at, emit_at):
    my_pair, my_ring, my_core = place[0], place[1], place[2]
    ring = n_row // 2
    step_of = -(-65536 // tiles)
    r = recv_list[...]
    q = (r * step_of) >> 16
    side = (q >= ring).astype(jnp.int32) ^ my_pair
    recv_at[...] = (((my_ring - q) & (ring - 1)) * 2 + side) * tiles + r - q * tiles
    e = emit_list[...]
    c = (e * step_of) >> 16
    emit_at[...] = ((c >> 1) + ((c ^ my_core) & 1) * (n_col // 2)) * tiles + e - c * tiles
    sub = lax.broadcasted_iota(jnp.int32, (LANES, LANES), 0)
    lane = lax.broadcasted_iota(jnp.int32, (LANES, LANES), 1)
    upper = jnp.concatenate([(sub < lane).astype(BF16), jnp.ones((LANES, LANES), BF16)], 1)
    carry = jnp.zeros((LANES, LANES), F32)
    found = jnp.zeros((LANES, 2 * LANES), F32)
    for g in range(tiles):
        named = owner[g : g + 1, :] == sub
        hot = jnp.where(named, 1.0, 0.0)
        counts = jnp.dot(hot.astype(BF16), upper, preferred_element_type=F32)
        place = jnp.sum(hot * (counts[:, :LANES] + carry), axis=0, keepdims=True)
        carry = carry + counts[:, LANES:]
        place = place.astype(jnp.int32)
        rank[g : g + 1, :] = place
        index = elem[g : g + 1, :]
        high = (index >> 7).astype(F32)
        low = (index & 127).astype(F32)
        at = place == sub
        table = jnp.concatenate([jnp.where(at, high, 0.0), jnp.where(at, low, 0.0)], 0)
        found = found + lax.dot_general(
            hot.astype(BF16), table.astype(BF16), NT, preferred_element_type=F32
        )
    slots[...] = found[:, :LANES] * 128.0 + found[:, LANES:]
    lanes = lax.broadcasted_iota(jnp.int32, (8, LANES), 1)
    subs = lax.broadcasted_iota(jnp.int32, (8, LANES), 0)
    total = jnp.zeros((8, LANES), F32)
    at = 0
    for i in range(8):
        sums = jnp.zeros((8, LANES), F32)
        for g in range(tiles):
            block = basis[:, g * LANES : (g + 1) * LANES]
            sums = sums + block * block[i : i + 1]
        value = jnp.sum(sums, axis=1, keepdims=True)
        total = total + jnp.where((subs >= i) & (lanes == at + subs - i), value, 0.0)
        at += 8 - i
    gram[...] = jnp.sum(total, axis=0, keepdims=True)


def receiver_kernel(*refs):
    wtab, features = refs[-2:]
    row = lax.broadcasted_iota(jnp.int32, (8, LANES), 0)
    zero = jnp.zeros((8, LANES), F32)
    base = 0
    for recv in refs[:-2]:
        blocks = recv.shape[0] // 6
        x = [recv[f * blocks : (f + 1) * blocks, :] for f in range(6)]
        x.append(-(x[0] * x[3] + x[1] * x[4] + x[2] * x[5]))
        x.append(x[0] * x[0] + x[1] * x[1] + x[2] * x[2])
        for f in range(8):
            features[pl.ds(f, blocks, stride=8), :] = x[f]

        def body(k, _):
            block = features[pl.ds(pl.multiple_of(k * 8, 8), 8), :]
            parts = split3(block)
            facing, away, spread = [], [], []
            for p, part in enumerate(parts):
                one = 1.0 if p == 0 else 0.0
                x_low = pltpu.roll(part, 3, 0)
                facing.append(jnp.where(row < 3, pltpu.roll(part, 5, 0), 0.0))
                away.append(jnp.where((row >= 3) & (row < 6), x_low, 0.0))
                spread.append(jnp.where(row < 3, -2.0 * part, jnp.where(row == 6, one, 0.0)))
            consts = []
            for f in (6, 7):
                h, m, l = (part[f : f + 1, :] for part in parts)
                consts.append(
                    jnp.where(row == 0, h, jnp.where(row == 1, m, jnp.where(row == 2, l, 0.0)))
                )
            ones = jnp.where((row >= 3) & (row < 6), 1.0, 0.0)
            for p, (w, c) in enumerate(
                ((facing, consts[0]), (away, ones), (spread, consts[1]))
            ):
                h, m, l = w
                wtab[base + k, :, p * LANES : (p + 1) * LANES] = jnp.concatenate(
                    [h, m, h, l, h, m, c, zero], 0
                ).astype(BF16)
            return 0

        lax.fori_loop(0, blocks, body, 0, unroll=8)
        base += blocks


def pair_kernel(tiles, n_row, n_col, unroll, count, recv_list, emit_list, place, near, far, wtab, out, etab, along, ratio, acc):
    row = lax.broadcasted_iota(jnp.int32, (8, LANES), 0)
    ones3 = jnp.where(row < 3, 1.0, 0.0)
    half = n_col // 2
    blocks = half * tiles
    ratios = []
    for s, source in enumerate((near, far)):
        feature = [source[pl.ds(f, blocks, stride=8), :] for f in range(8)]
        ratios.append(feature[7])
        total = -(feature[0] * feature[3] + feature[1] * feature[4] + feature[2] * feature[5])
        for p, part in enumerate(split3(total)):
            along[p, s * blocks : (s + 1) * blocks, :] = part
    ratios = jnp.concatenate(ratios, 0)
    for k in range(2 * blocks // LANES):
        ratio[k] = ratios[k * LANES : (k + 1) * LANES].T
    for s, source in enumerate((near, far)):

        def body(g, _):
            for k in range(tiles):
                at = g * tiles + k
                h, m, l = split3(source[pl.ds(pl.multiple_of(at * 8, 8), 8), :])
                ph, pm, pl_ = (along[p, pl.ds(s * blocks + at, 1), :] for p in range(3))
                tail = jnp.where(
                    row < 3,
                    1.0,
                    jnp.where(
                        row == 3, ph, jnp.where(row == 4, pm, jnp.where(row == 5, pl_, 0.0))
                    ),
                )
                etab[s * blocks + at] = jnp.concatenate(
                    [h, h, m, h, l, m, tail, jnp.zeros_like(tail)], 0
                ).astype(BF16)
            return 0

        lax.fori_loop(0, half, body, 0)
    acc[...] = jnp.zeros_like(acc)
    live = count[0]

    def fold(full):
        total = full[0:8]
        for k in range(1, LANES // 8):
            total = total + full[8 * k : 8 * k + 8]
        return total

    my_pair, my_ring = place[0], place[1]
    ring = n_row // 2

    empty = jnp.zeros((64, 3 * LANES), BF16)

    def view(g, e):
        facing = jnp.maximum(g[:, :LANES], 0.0)
        away = jnp.maximum(g[:, LANES : 2 * LANES], 0.0)
        spread = g[:, 2 * LANES :]
        first = facing * away / (spread * spread)
        lane = jnp.full((LANES, LANES), e & (LANES - 1), jnp.int32)
        factor = jnp.take_along_axis(ratio[e >> 7], lane, axis=1, mode="promise_in_bounds")
        return fold(first), fold(first * factor)

    def two(at):
        r = recv_list[at], recv_list[at + 1]
        e = emit_list[at], emit_list[at + 1]
        weights = jnp.concatenate(
            [
                jnp.concatenate([wtab[r[0]], empty], 0),
                jnp.concatenate([empty, wtab[r[1]]], 0),
            ],
            1,
        )
        g = lax.dot_general(
            jnp.concatenate([etab[e[0]], etab[e[1]]], 0), weights, TN, preferred_element_type=F32
        )
        return [
            (r[k],) + view(g[:, 3 * k * LANES : 3 * (k + 1) * LANES], e[k]) for k in range(2)
        ]

    def step(i, _):
        found = []
        for k in range(0, unroll, 2):
            found += two(i * unroll + k)
        for k, (r, first, second) in enumerate(found):
            keep = jnp.where(i * unroll + k < live, 1.0, 0.0)
            at = pl.multiple_of(r * 16, 16)
            acc[pl.ds(at, 8), :] = acc[pl.ds(at, 8), :] + first * keep
            acc[pl.ds(at + 8, 8), :] = acc[pl.ds(at + 8, 8), :] + second * keep
        return 0

    lax.fori_loop(0, (live + unroll - 1) // unroll, step, 0)
    for q in range(n_row):
        target = (my_pair ^ (q & 1)) * ring + ((my_ring - (q >> 1)) & (ring - 1))
        for v in range(2):
            total = acc[pl.ds(q * tiles * 16 + v * 8, tiles, stride=16), :]
            for s in range(1, 8):
                total = total + acc[pl.ds(q * tiles * 16 + v * 8 + s, tiles, stride=16), :]
            at = pl.multiple_of((target * 2 + v) * tiles, 8)
            out[pl.ds(at, tiles), :] = total


def load_kernel(tiles, n_row, part, basis, mirrored, inner, area, owner, rank, slots, gram, message, damped):
    sub = lax.broadcasted_iota(jnp.int32, (LANES, LANES), 0)
    irradiance = part[0:tiles, :]
    scattered = part[tiles : 2 * tiles, :]
    for q in range(1, n_row):
        irradiance = irradiance + part[2 * q * tiles : (2 * q + 1) * tiles, :]
        scattered = scattered + part[(2 * q + 1) * tiles : (2 * q + 2) * tiles, :]
    fraction = mirrored[...]
    lost = fraction * scattered
    damped[...] = lost
    power = (1.0 - fraction) * irradiance + inner[...]
    load = 20.0 * area[...] * jnp.sqrt(jnp.sqrt(power))
    parts = split3(load)
    found = jnp.zeros((LANES, LANES), F32)
    for begin in range(0, tiles, 4):
        hots, tables = [], []
        for g in range(begin, begin + 4):
            hots += [jnp.where(owner[g : g + 1, :] == sub, 1.0, 0.0).astype(BF16)] * 3
            at = rank[g : g + 1, :] == sub
            tables += [jnp.where(at, v[g : g + 1, :], 0.0).astype(BF16) for v in parts]
        found = found + lax.dot_general(
            jnp.concatenate(hots, 1), jnp.concatenate(tables, 1), NT, preferred_element_type=F32
        )
    lanes = lax.broadcasted_iota(jnp.int32, (8, LANES), 1)
    subs = lax.broadcasted_iota(jnp.int32, (8, LANES), 0)
    sums = jnp.zeros((8, LANES), F32)
    for g in range(tiles):
        sums = sums + basis[:, g * LANES : (g + 1) * LANES] * lost[g : g + 1, :]
    inner_products = jnp.sum(sums, axis=1, keepdims=True)
    square = jnp.sum(lost * lost, axis=(0, 1), keepdims=True)
    stats = jnp.sum(
        jnp.where(lanes == 96 + subs, inner_products, 0.0), axis=0, keepdims=True
    )
    g = jnp.broadcast_to(gram[...], (8, LANES))
    lane = lanes[0:1]
    stats = jnp.where(lane == 104, square, stats)
    stats = jnp.where(lane >= 105, pltpu.roll(g, 105, 1)[0:1], stats)
    more = pltpu.roll(g, 73, 1)[0:1]
    keep = lax.broadcasted_iota(jnp.int32, (LANES, LANES), 1) < 96
    message[pl.ds(0, LANES, stride=2), :] = jnp.where(keep, found, stats)
    message[pl.ds(1, LANES, stride=2), :] = jnp.where(keep, slots[...], more)


def finish_kernel(tiles, cells, arrived, basis, damped, vector, hessen, loads, value_rows, high_rows, low_rows):
    values = arrived[pl.ds(0, LANES, stride=2), :]
    second = arrived[pl.ds(1, LANES, stride=2), :]
    top = jnp.sum(values, axis=0, keepdims=True)
    low = jnp.sum(second, axis=0, keepdims=True)
    inner = [top[:, 96 + k : 97 + k] for k in range(8)]
    lost_square = top[:, 104:105]
    gram = {}
    at = 0
    for i in range(8):
        for j in range(i, 8):
            lane = 105 + at
            gram[i, j] = top[:, lane : lane + 1] if lane < 128 else low[:, lane - 32 : lane - 31]
            gram[j, i] = gram[i, j]
            at += 1
    scale = 1.0 / cells
    coeffs = [(gram[7, k] - inner[k]) * scale for k in range(8)]
    left = [(1.0 if k == 7 else 0.0) - coeffs[k] for k in range(8)]
    square = lost_square
    for i in range(8):
        line = gram[i, i] * left[i] - 2.0 * inner[i]
        for j in range(i + 1, 8):
            line = line + 2.0 * gram[i, j] * left[j]
        square = square + line * left[i]
    length = jnp.sqrt(jnp.maximum(square, 0.0) * scale + 1e-6)
    inverse = 1.0 / length
    subs = lax.broadcasted_iota(jnp.int32, (8, LANES), 0)
    weights = jnp.zeros((8, LANES), F32)
    for k in range(8):
        weights = jnp.where(subs == k, left[k], weights)
    for g in range(tiles):
        mixed = jnp.sum(basis[:, g * LANES : (g + 1) * LANES] * weights, axis=0, keepdims=True)
        vector[g : g + 1, :] = (mixed - damped[g : g + 1, :]) * inverse
    lanes = lax.broadcasted_iota(jnp.int32, (1, LANES), 1)
    column = jnp.where(lanes == 8, length, 0.0)
    for k in range(8):
        column = jnp.where(lanes == k, coeffs[k], column)
    hessen[...] = column[:, 0:9]
    keep = lax.broadcasted_iota(jnp.int32, (LANES, LANES), 1) < 96
    for k, v in enumerate(split3(jnp.where(keep, values, 0.0))):
        value_rows[k] = v
    index = second.astype(jnp.int32)
    high_rows[...] = (index >> 7).astype(F32)
    low_rows[...] = (index & 127).astype(F32)
    sub = lax.broadcasted_iota(jnp.int32, (LANES, LANES), 0).astype(F32).astype(BF16)
    sub16 = sub[0:16]
    one, none = jnp.ones((16, LANES), BF16), jnp.zeros((16, LANES), BF16)

    def wide(row):
        return jnp.broadcast_to(row, (16, LANES)).astype(BF16)

    total = jnp.zeros((LANES, 48), F32)
    for s in range(0, LANES, 8):
        left_side, right_side = [], []
        for u in range(s, s + 8):
            high = wide(high_rows[u : u + 1, :])
            low = wide(low_rows[u : u + 1, :])
            mask = high == sub16
            left_side.append(
                jnp.concatenate(
                    [
                        jnp.where(mask, wide(value_rows[k, u : u + 1, :]), none)
                        for k in range(3)
                    ],
                    0,
                )
            )
            right_side.append(
                jnp.concatenate(
                    [
                        jnp.where(low == sub[k : k + 16], one, none)
                        for k in range(0, LANES, 16)
                    ],
                    0,
                )
            )
        total = total + lax.dot_general(
            jnp.concatenate(right_side, 1),
            jnp.concatenate(left_side, 1),
            NT,
            preferred_element_type=F32,
        )
    total = total.T
    loads[...] = total[0:16] + total[16:32] + total[32:48]


def shards(
    positions,
    normals,
    patch_extents,
    mirrored_fraction,
    inner_emission_power,
    radiosity,
    basis,
    recv_blocks,
    emit_blocks,
    vis_count,
    owner,
    local_elem,
):
    patches = positions.shape[1]
    tiles = patches // LANES
    pairs_of, ring, half, cores = (lax.axis_size(a) for a in AXES)
    n_row, n_col = pairs_of * ring, half * cores
    devices = n_row * n_col
    place = jnp.stack([lax.axis_index(a) for a in ("pair", "ring", "core")])
    shape = jax.ShapeDtypeStruct

    def rows(array):
        return array.reshape(-1, LANES)

    hbm = pl.BlockSpec(memory_space=pl.ANY)
    swap = [(0, 1), (1, 0)]
    swapped = [lax.ppermute(array, "pair", swap) for array in (positions, normals)]
    emit = call(
        functools.partial(emit_kernel, tiles, half),
        shape((half * 8 * tiles, LANES), F32),
        scratch=[
            pltpu.VMEM((3, patches), F32),
            pltpu.VMEM((3, patches), F32),
            pltpu.VMEM((1, patches), F32),
            pltpu.VMEM((1, patches), F32),
            pltpu.VMEM((8, patches), F32),
            pltpu.SemaphoreType.DMA((5,)),
        ],
        in_specs=[hbm] * 5,
        name="emit",
        micros=4,
        limit=60 * 2**20,
    )(positions, normals, patch_extents[None], radiosity[None], basis)
    both = call(
        functools.partial(join_kernel, tiles),
        shape((12 * tiles, LANES), F32),
        in_specs=[VMEM] * 4,
        name="join",
        micros=3,
    )(positions, normals, *swapped)
    owner_rows, both_again = lax.optimization_barrier((rows(owner), both))
    lists = rows(recv_blocks), rows(emit_blocks)
    rank, slots, gram, recv_at, emit_at = call(
        functools.partial(rank_kernel, tiles, n_row, n_col),
        (
            shape((tiles, LANES), jnp.int32),
            shape((LANES, LANES), F32),
            shape((1, LANES), F32),
            shape(lists[0].shape, jnp.int32),
            shape(lists[1].shape, jnp.int32),
        ),
        in_specs=[SMEM] + [VMEM] * 5,
        name="rank",
        micros=3,
        limit=60 * 2**20,
    )(place, owner_rows, rows(local_elem), basis, *lists)
    received = [both_again] + [
        lax.ppermute(both, "ring", [(i, (i + k) % ring) for i in range(ring)])
        for k in range(1, ring)
    ]
    near = rows(lax.all_to_all(emit.reshape(half, -1), "half", 0, 0, tiled=True))
    near, received, recv_at, emit_at = lax.optimization_barrier(
        (near, received, recv_at, emit_at)
    )
    far = lax.ppermute(near, "core", [(0, 1), (1, 0)])
    wtab = call(
        receiver_kernel,
        shape((n_row * tiles, 64, 3 * LANES), BF16),
        scratch=[pltpu.VMEM((16 * tiles, LANES), F32)],
        in_specs=[VMEM] * len(received),
        name="receivers",
        micros=4,
    )(*received)
    unroll = 64
    part = call(
        functools.partial(pair_kernel, tiles, n_row, n_col, unroll),
        shape((n_row * 2 * tiles, LANES), F32),
        scratch=[
            pltpu.VMEM((n_col * tiles, 64, LANES), BF16),
            pltpu.VMEM((3, n_col * tiles, LANES), F32),
            pltpu.VMEM((n_col * tiles // LANES, LANES, LANES), F32),
            pltpu.VMEM((n_row * tiles * 16, LANES), F32),
        ],
        in_specs=[SMEM] * 4 + [VMEM] * 3,
        name="pairs",
        micros=20,
    )(
        vis_count.reshape(-1),
        recv_at.reshape(-1),
        emit_at.reshape(-1),
        place,
        near,
        far,
        wtab,
    )
    part = lax.all_to_all(part.reshape(n_row, -1), ROW, 0, 0, tiled=True)
    message, damped = call(
        functools.partial(load_kernel, tiles, n_row),
        (shape((2 * devices, LANES), F32), shape((tiles, LANES), F32)),
        in_specs=[VMEM] * 9,
        name="loads",
    )(
        rows(part),
        basis,
        rows(mirrored_fraction),
        rows(inner_emission_power),
        rows(patch_extents),
        owner_rows,
        rank,
        slots,
        gram,
    )
    arrived = lax.all_to_all(message.reshape(devices, -1), AXES, 0, 0, tiled=True)
    vector, hessen, loads = call(
        functools.partial(finish_kernel, tiles, float(patches * devices)),
        (
            shape((tiles, LANES), F32),
            shape((1, 9), F32),
            shape((E_DEV // LANES, LANES), F32),
        ),
        scratch=[pltpu.VMEM((3, LANES, LANES), F32)] + [pltpu.VMEM((LANES, LANES), F32)] * 2,
        in_specs=[VMEM] * 3,
        name="finish",
    )(rows(arrived), basis, damped)
    return vector.reshape(-1), hessen.reshape(-1), loads.reshape(-1)


def solution(mesh):
    n_row, n_col = mesh.shape["row"], mesh.shape["col"]
    fine = Mesh(mesh.devices.reshape(2, n_row // 2, n_col // 2, 2), AXES)
    every = P(AXES)
    second = P(None, AXES)
    grid = P(ROW, ("half", "core"))
    in_specs = (
        second,
        second,
        every,
        every,
        every,
        every,
        second,
        P(ROW, ("half", "core"), None),
        P(ROW, ("half", "core"), None),
        grid,
        P(AXES, None),
        every,
    )
    return jax.shard_map(
        shards, mesh=fine, in_specs=in_specs, out_specs=(every, P(), every), check_vma=False
    )
```
